32 devices in a mesh: dp: 8 (over z, y), seq: 4 (over x, core).
Axes of the slice: x: 2, y: 2, z: 4, core: 2. Of those that a mesh axis runs over, the one named last changes fastest.
Arguments:
- tokens: bfloat16 [32, 256, 768], P('dp', 'seq'), may hold values from -6 to 6
- pad_mask: int32 [32, 256], P('dp'), may hold values from 0 to 1, as said below
- counts: int32 [8], P('dp'), may hold values from 2 to 4, as said below
- attn_gain: bfloat16 [768], P('dp'), may hold values from 0.5 to 1.5
- attn_shift: bfloat16 [768], P('dp'), may hold values from -4 to 4
- qkv_weight: bfloat16 [768, 2304], P('dp'), may hold values from -0.21875 to 0.21875
- mix_weight: bfloat16 [768, 768], P('dp'), may hold values from -1.75 to 1.75
- mix_bias: bfloat16 [768], P('dp'), may hold values from -4 to 4
- moe_gain: bfloat16 [768], P('dp'), may hold values from 0.5 to 1.5
- moe_shift: bfloat16 [768], P('dp'), may hold values from -4 to 4
- router: bfloat16 [768, 32], P('dp'), may hold values from -0.109375 to 0.109375
- expert_in: bfloat16 [32, 768, 3072], P(('dp', 'seq')), may hold values from -2.5 to 2.5
- hidden_bias: bfloat16 [32, 3072], P(('dp', 'seq')), may hold values from -1.5 to 1.5
- expert_out: bfloat16 [32, 3072, 768], P(('dp', 'seq')), may hold values from -1.75 to 1.75
- output_bias: bfloat16 [32, 768], P(('dp', 'seq')), may hold values from -6 to 6
- cotangent: bfloat16 [32, 256, 768], P('dp', 'seq'), may hold values from -6 to 6
Outputs:
- block_out: bfloat16 [32, 256, 768], P('dp', 'seq')
- input_grad: bfloat16 [32, 256, 768], P('dp', 'seq')
- grad_attn_gain: float32 [768], P('dp')
- grad_attn_shift: float32 [768], P('dp')
- grad_qkv_weight: float32 [768, 2304], P('dp')
- grad_mix_weight: float32 [768, 768], P('dp')
- grad_mix_bias: float32 [768], P('dp')
- grad_moe_gain: float32 [768], P('dp')
- grad_moe_shift: float32 [768], P('dp')
- grad_router: float32 [768, 32], P('dp')
- grad_expert_in: float32 [32, 768, 3072], P(('dp', 'seq'))
- grad_hidden_bias: float32 [32, 3072], P(('dp', 'seq'))
- grad_expert_out: float32 [32, 3072, 768], P(('dp', 'seq'))
- grad_output_bias: float32 [32, 768], P(('dp', 'seq'))
The draws below stay inside these ranges and needn't reach their ends.
Inputs may be any that keep to these rules, and one draw needn't show every extreme that they name: `pad_mask`: each image's mask is 1 on its first tokens, between 193 and 197 of them, and 0 after. Index d of dp holds counts[d] live images in its first image slots; its other slots are padding; some index is full.
All inputs are finite; a program needn't handle non-finite values.
Results may differ from the reference program's by a relative error of at most 0.018.
Values may be sent and summed in bfloat16 or wider, within the bound.
No kernel may reach another device: no remote copies, remote signals or barrier semaphores. Data moves between devices by JAX's collectives and lax.ppermute only.
A program may use at most 128 MiB of HBM per device.

```python
import jax
import jax.numpy as jnp
from jax import lax

D = 768
HEADS = 12
HEAD_DIM = 64
FF = 3072
IMG_CAP = 4
PADLEN = 256
MAXREAL = 197
EXPERTS = 32
SHARD_TOK = 64
IMAGES = 32
N_DP = 8


def draw_pad_mask(key, part):
    key = jax.random.fold_in(key, 11)
    lengths = jax.random.randint(key, (IMAGES, 1), PADLEN - SHARD_TOK + 1, MAXREAL + 1)
    return (jnp.arange(PADLEN, dtype=jnp.int32)[None, :] < lengths).astype(jnp.int32)


def draw_counts(key, part):
    key = jax.random.fold_in(key, 23)
    first, second = jax.random.split(key)
    loads = jax.random.randint(first, (N_DP,), IMG_CAP // 2, IMG_CAP + 1)
    fullest = jax.random.randint(second, (), 0, N_DP)
    return loads.at[fullest].set(IMG_CAP).astype(jnp.int32)


def draw_output_bias(key, part):
    key = jax.random.fold_in(key, 37)
    rows_key, shared_key = jax.random.split(key)
    rows = jax.random.normal(rows_key, (EXPERTS, D), jnp.float32)
    shared = 0.5 * jax.random.normal(shared_key, (1, D), jnp.float32)
    return jnp.clip(rows + shared, -6.0, 6.0).astype(jnp.bfloat16)


def shard_levels(key, extent, cuts, least, top_value):
    level = 1.0
    for position, shards_of in cuts:
        draws = jax.random.uniform(jax.random.fold_in(jax.random.fold_in(key, 6), position), (shards_of,), jnp.float32, least / len(cuts), top_value / len(cuts))
        level = level * jnp.repeat(jnp.exp(draws), extent[position] // shards_of).reshape((-1,) + (1,) * (len(extent) - 1 - position))
    return level


def noise(key, shape, width, reach, cuts=(), kind=jnp.bfloat16):
    drawn = jax.random.normal(key, shape, jnp.float32) * width
    if len(cuts) > 0:
        drawn = shard_levels(key, shape, cuts, -0.22, 0.18) * drawn
    return jnp.clip(drawn, min=-reach, max=reach).astype(kind)


def setup_inputs(seed: int = 0) -> dict:
    key_list = jax.random.split(jax.random.key(seed), 17)
    return {
        "tokens": noise(key_list[0], (IMAGES, PADLEN, D), 1.0, 6.0, ((0, 8), (1, 4))),
        "pad_mask": draw_pad_mask(jax.random.fold_in(key_list[16], 71), 0),
        "counts": draw_counts(jax.random.fold_in(key_list[16], 71), 0),
        "attn_gain": jnp.clip(1.0 + 0.1 * jax.random.normal(key_list[3], (D,), jnp.float32), 0.5, 1.5).astype(jnp.bfloat16),
        "attn_shift": noise(key_list[4], (D,), 0.3, 4.0, ((0, 8),)),
        "qkv_weight": noise(key_list[5], (D, 3 * D), D ** -0.5, 0.21875, ((0, 8),)),
        "mix_weight": noise(key_list[6], (D, D), (max(D // 64, 1)) ** -0.5, 1.75, ((0, 8),)),
        "mix_bias": noise(key_list[7], (D,), 0.3, 4.0, ((0, 8),)),
        "moe_gain": jnp.clip(1.0 + 0.1 * jax.random.normal(key_list[8], (D,), jnp.float32), 0.5, 1.5).astype(jnp.bfloat16),
        "moe_shift": noise(key_list[9], (D,), 0.3, 4.0, ((0, 8),)),
        "router": noise(key_list[10], (D, EXPERTS), (4 * D) ** -0.5, 0.109375, ((0, 8),)),
        "expert_in": noise(key_list[11], (EXPERTS, D, FF), (max(D // 128, 1)) ** -0.5, 2.5, ((0, 32),)),
        "hidden_bias": noise(key_list[12], (EXPERTS, FF), 0.1, 1.5, ((0, 32),)),
        "expert_out": noise(key_list[13], (EXPERTS, FF, D), (max(FF // 256, 1)) ** -0.5, 1.75, ((0, 32),)),
        "output_bias": draw_output_bias(jax.random.fold_in(key_list[16], 71), 0),
        "cotangent": noise(key_list[15], (IMAGES, PADLEN, D), 1.0, 6.0, ((0, 8), (1, 4))),
    }


@jax.custom_vjp
def low(v):
    return lax.optimization_barrier(v.astype(jnp.bfloat16)).astype(jnp.float32)

@jax.custom_vjp
def low_back(v):
    return v

def low_keep(v):
    return (low(v), None)

def low_pass(kept, grad):
    return (grad,)

def back_keep(v):
    return (v, None)

def back_low(kept, grad):
    return (low(grad),)
low.defvjp(low_keep, low_pass)
low_back.defvjp(back_keep, back_low)
highest = lax.Precision.HIGHEST
eps_norm = 1e-06

def normalize(values, gain_row, shift_row):
    center = values - lax.optimization_barrier(jnp.mean(values, axis=-1, keepdims=True))
    spread = lax.optimization_barrier(jnp.mean(center * center, axis=-1, keepdims=True))
    return center * lax.rsqrt(spread + eps_norm) * gain_row + shift_row

def forward(tokens, attn_gain, attn_shift, qkv_weight, mix_weight, mix_bias, moe_gain, moe_shift, router, expert_in, hidden_bias, expert_out, output_bias, valid_rows):
    scaling = HEAD_DIM ** (-0.5)
    token_groups = tokens.reshape(N_DP, IMG_CAP, PADLEN, D)
    valid_groups = valid_rows.reshape(N_DP, IMG_CAP, PADLEN)

    def section_one(pieces):
        image_block, live_rows = pieces
        normed = low(normalize(image_block, attn_gain, attn_shift))
        project = low(low_back(jnp.einsum('itd,df->itf', normed, qkv_weight, precision=highest)))
        project = project.reshape(IMG_CAP, PADLEN, 3, HEADS, HEAD_DIM)
        queries = project[:, :, 0]
        key_rows = project[:, :, 1]
        values = project[:, :, 2]
        scores = low_back(jnp.einsum('iqhd,ikhd->ihqk', queries, key_rows, precision=highest) * scaling)
        scores = jnp.where(live_rows[:, None, None, :] > 0, scores, -1000000000.0)
        attn_probs = low(jax.nn.softmax(scores, axis=-1))
        heads_out = low(low_back(jnp.einsum('ihqk,ikhd->iqhd', attn_probs, values, precision=highest)))
        heads_out = heads_out.reshape(IMG_CAP, PADLEN, D)
        resid = image_block + jnp.einsum('itd,de->ite', heads_out, mix_weight, precision=highest) + mix_bias
        mixed = low(normalize(resid, moe_gain, moe_shift))
        logits = low_back(jnp.einsum('itd,de->ite', mixed, router, precision=highest))
        masked = jnp.where(live_rows[:, :, None] > 0, logits, -1000000000.0)
        dispatch = low(jax.nn.softmax(masked, axis=1))
        slots = jnp.einsum('ite,itd->ied', dispatch, mixed, precision=highest)
        return (resid, logits, slots)
    resid, logits, slots = lax.map(jax.checkpoint(section_one), (token_groups, valid_groups))
    slots = low(low_back(slots)).reshape(IMAGES, EXPERTS, D)
    by_expert = jnp.transpose(slots, (1, 0, 2))

    def run_expert(pieces):
        inputs, first_weight, first_bias, second_weight, second_bias = pieces
        pre_act = low_back(jnp.dot(inputs, first_weight, precision=highest) + first_bias)
        hidden = low(jax.nn.gelu(pre_act, approximate=False))
        return low(low_back(jnp.dot(hidden, second_weight, precision=highest) + second_bias))
    results = lax.map(jax.checkpoint(run_expert), (by_expert, expert_in, hidden_bias, expert_out, output_bias))
    results = jnp.transpose(results, (1, 0, 2)).reshape(N_DP, IMG_CAP, EXPERTS, D)

    def section_two(pieces):
        resid_block, logit_block, result_block, live_rows = pieces
        combine = low(jax.nn.softmax(logit_block, axis=-1))
        moe_out = jnp.einsum('ite,ied->itd', combine, result_block, precision=highest)
        return (resid_block + moe_out) * live_rows[:, :, None]
    outputs = lax.map(jax.checkpoint(section_two), (resid, logits, results, valid_groups))
    return outputs.reshape(IMAGES, PADLEN, D)

def reference(tokens, pad_mask, counts, attn_gain, attn_shift, qkv_weight, mix_weight, mix_bias, moe_gain, moe_shift, router, expert_in, hidden_bias, expert_out, output_bias, cotangent):
    live_slots = (jnp.arange(IMG_CAP, dtype=jnp.int32)[None, :] < counts[:, None]).reshape(IMAGES)
    valid_rows = (pad_mask * live_slots[:, None].astype(jnp.int32)).astype(jnp.float32)
    params = tuple((item.astype(jnp.float32) for item in (tokens, attn_gain, attn_shift, qkv_weight, mix_weight, mix_bias, moe_gain, moe_shift, router, expert_in, hidden_bias, expert_out, output_bias)))

    def wrapped(*items):
        return forward(*items, valid_rows)
    outputs, pullback = jax.vjp(wrapped, *params)
    grads = pullback(cotangent.astype(jnp.float32))
    return (outputs.astype(jnp.bfloat16), grads[0].astype(jnp.bfloat16), grads[1], grads[2], grads[3], grads[4], grads[5], grads[6], grads[7], grads[8], grads[9], grads[10], grads[11], grads[12])
```

```python
import math

import jax
import jax.numpy as jnp
from jax import lax
from jax.experimental import pallas as pl
from jax.experimental.pallas import tpu as pltpu
from jax.sharding import PartitionSpec as P

HEADS = 12
HEAD_DIM = 64
EPS = 1e-06
NEG = -1000000000.0
BF16 = jnp.bfloat16
F32 = jnp.float32
ALL_VMEM = 62.6
FOLD = 112
ROWS = 208
NT = (((1,), (1,)), ((), ()))
TN = (((0,), (0,)), ((), ()))


def mm(a, b):
    return jnp.dot(a, b, preferred_element_type=F32)


def mm_nt(a, b):
    return lax.dot_general(a, b, NT, preferred_element_type=F32)


def mm_tn(a, b):
    return lax.dot_general(a, b, TN, preferred_element_type=F32)


def unit(values):
    center = values - jnp.mean(values, axis=-1, keepdims=True)
    spread = jnp.mean(center * center, axis=-1, keepdims=True)
    root = lax.rsqrt(spread + EPS)
    return center * root, root


def unit_back(scaled, rows, root):
    inner = jnp.mean(scaled * rows, axis=-1, keepdims=True)
    return root * (scaled - jnp.mean(scaled, axis=-1, keepdims=True) - rows * inner)


def lane_mask(index, width):
    lane = lax.broadcasted_iota(jnp.int32, (1, width), 1)
    return (lane >= index * HEAD_DIM) & (lane < (index + 1) * HEAD_DIM)


def image_length(mask_ref, counts_ref, image):
    which = lax.broadcasted_iota(jnp.int32, mask_ref.shape, 0)
    real = jnp.where(which == image, mask_ref[...], 0)
    total = jnp.sum(jnp.sum(real, axis=1, keepdims=True), axis=0, keepdims=True)
    return jnp.where(image < counts_ref[0], total, 0)


def kernel_call(
    kernel, ins, outs, scratch=(), limit=48, smem=(), hbm_in=(), hbm_out=(), aliases=None, flops=1
):
    kw = {
        "input_output_aliases": aliases or {},
        "cost_estimate": pl.CostEstimate(flops=int(flops), bytes_accessed=0, transcendentals=0),
    }
    n_in, n_out, n_own = len(ins), len(outs), len(scratch)
    n_staged = len(hbm_in) + len(hbm_out)

    def wrapped(*refs):
        in_refs = list(refs[:n_in])
        out_refs = list(refs[n_in : n_in + n_out])
        own = refs[n_in + n_out : n_in + n_out + n_own]
        stages = refs[n_in + n_out + n_own :]
        reads, writes = [], {}
        for j, i in enumerate(hbm_in):
            reads.append(pltpu.make_async_copy(in_refs[i], stages[j], stages[-1].at[j]))
            in_refs[i] = stages[j]
        for j, i in enumerate(hbm_out, len(hbm_in)):
            writes[i] = pltpu.make_async_copy(stages[j], out_refs[i], stages[-1].at[j])
            out_refs[i] = stages[j]
        for copy in reads:
            copy.start()
        for copy in reads:
            copy.wait()
        kernel(*in_refs, *out_refs, *own)
        for copy in writes.values():
            copy.start()
        for copy in writes.values():
            copy.wait()

    def spec(i, staged):
        if i in staged:
            return pl.BlockSpec(memory_space=pltpu.HBM)
        return pl.BlockSpec(memory_space=pltpu.VMEM)

    in_specs = [
        pl.BlockSpec(memory_space=pltpu.SMEM) if i in smem else spec(i, hbm_in)
        for i in range(n_in)
    ]
    scratch = list(scratch)
    scratch += [pltpu.VMEM(ins[i].shape, ins[i].dtype) for i in hbm_in]
    scratch += [pltpu.VMEM(*outs[i]) for i in hbm_out]
    if n_staged:
        scratch.append(pltpu.SemaphoreType.DMA((n_staged,)))
    call = pl.pallas_call(
        wrapped,
        in_specs=in_specs,
        out_specs=[spec(i, hbm_out) for i in range(n_out)],
        out_shape=[jax.ShapeDtypeStruct(shape, kind) for shape, kind in outs],
        scratch_shapes=scratch,
        compiler_params=pltpu.CompilerParams(vmem_limit_bytes=int(limit * 2**20)),
        **kw,
    )
    return list(call(*ins))


def place(full, refs, dp):
    if len(refs) == 1:
        full[...] = refs[0][...]
        return
    part = refs[0].shape[0]
    half = part // 2

    def put(ref, rows, step, lo):
        at = pl.multiple_of((dp ^ step) * part + lo, half)
        full[pl.ds(at, rows.stop - rows.start), :] = ref[rows, :]

    whole, rest = slice(0, part), slice(part, part + half)
    for ref, step in zip(refs, (0, 1, 2, 4, 5, 6)):
        put(ref, whole, step, 0)
    put(refs[4], rest, 3, 0)
    put(refs[5], rest, 3, half)
    put(refs[6], slice(0, half), 7, 0)
    put(refs[7], slice(0, half), 7, half)


def forward_blocks(beside, across, far, y_ref, z_ref):
    part = far.shape[0]
    half = part // 2
    y_ref[:part, :] = far[...]
    y_ref[part:, :] = across[:half, :]
    z_ref[:part, :] = far[...]
    z_ref[part:, :] = beside[half:, :]


def forward_last(y_ref, z_ref, first_ref, second_ref):
    half = first_ref.shape[0]
    first_ref[...] = z_ref[:half, :]
    second_ref[...] = y_ref[half : 2 * half, :]


def head_masks(width, heads_here):
    return [lane_mask(h, width) for h in range(heads_here)]


def pack_inputs(groups, here, half, misc_w, experts):
    def kernel(*refs):
        qkv_ref, router_ref = refs[:2]
        vectors = refs[2:7]
        mix_ref, cot_ref, piece_ref = refs[7:10]
        cot_refs = refs[10 : 10 + groups]
        turn = refs[-1]
        seq = lax.axis_index("seq")
        features = qkv_ref.shape[1] // 3
        part = qkv_ref.shape[0]
        for g in range(groups):

            @pl.when(seq == g)
            def _():
                for j in range(3):
                    lo = j * features + g * here
                    piece_ref[:, j * here : (j + 1) * here] = qkv_ref[:, lo : lo + here]

        turn[...] = jnp.zeros_like(turn)
        turn[:experts, :part] = router_ref[...].astype(F32)
        for j in range(5):
            turn[experts + j : experts + j + 1, :part] = vectors[j][...].astype(F32)
        lo = 3 * here + misc_w
        piece_ref[:, 3 * here : lo] = turn[...].T[:part].astype(BF16)
        piece_ref[:, lo:] = mix_ref[:, pl.ds(pl.multiple_of((seq & 1) * half, 128), half)]
        for r in range(groups):
            cot_refs[r][...] = cot_ref[pl.ds(seq ^ r, 1)][0]

    return kernel


def normalize_tokens(groups):
    def kernel(*refs):
        tok_refs = refs[:groups]
        normed_ref, unit_ref, mine_ref, tok = refs[groups:]
        seq = lax.axis_index("seq")
        images, shard, _ = tok_refs[0].shape
        for r in range(groups):
            rows = pl.ds(pl.multiple_of((seq ^ r) * shard, shard), shard)
            tok[:, rows, :] = tok_refs[r][...]
        mine_ref[...] = tok[pl.ds(seq, 1), :ROWS, :][0]
        for i in range(images):
            normed, _ = unit(tok[i, :ROWS, :].astype(F32))
            normed_ref[i] = normed
            unit_ref[i] = normed.astype(BF16)

    return kernel


def attend_forward(groups, pieces, here, wide, misc_w, experts):
    heads_here = HEADS // groups

    def kernel(*refs):
        normed_ref, mask_ref, counts_ref = refs[:3]
        w_refs = refs[3 : 3 + pieces]
        sent_refs = refs[3 + pieces : 3 + pieces + groups]
        rest = refs[3 + pieces + groups :]
        (half_ref, probs_ref, xa_ref, qkv_ref, wpad_ref, rows_ref, router_ref, dense, heads) = rest
        seq = lax.axis_index("seq")
        images, _, features = normed_ref.shape
        place(dense, w_refs, lax.axis_index("dp"))
        wpad_ref[...] = jnp.zeros_like(wpad_ref)
        for j in range(3):
            wpad_ref[:, j * wide : j * wide + here] = dense[:, j * here : (j + 1) * here]
        half_ref[...] = dense[:, 3 * here + misc_w :]
        misc = dense[:, 3 * here : 3 * here + misc_w]
        router_ref[...] = misc[:, :experts]
        rows_ref[...] = misc.astype(F32).T[experts : experts + 8]
        xa_ref[...] = (normed_ref[...] * rows_ref[0:1][None] + rows_ref[1:2][None]).astype(BF16)
        flat = xa_ref[...].reshape(images * ROWS, features)
        qkv_ref[:, :ROWS, :] = (
            mm(flat, wpad_ref[...]).astype(BF16).reshape(images, ROWS, 3 * wide)
        )
        keys = qkv_ref.shape[1]
        qkv_ref[:, ROWS:, :] = jnp.zeros((images, keys - ROWS, 3 * wide), BF16)
        place_of_key = lax.broadcasted_iota(jnp.int32, (1, keys), 1)
        for i in range(images):
            valid = place_of_key < image_length(mask_ref, counts_ref, i)
            q, k, v = head_stacks(qkv_ref, i, wide, heads_here)
            scores = mm_nt(q, k) * HEAD_DIM ** (-0.5)
            for h in range(heads_here):
                lanes = slice(h * keys, (h + 1) * keys)
                masked = jnp.where(valid, scores[:, lanes], NEG)
                top = jnp.exp(masked - jnp.max(masked, axis=-1, keepdims=True))
                total = jnp.sum(top, axis=-1, keepdims=True)
                probs_ref[i, :, lanes] = (top / total).astype(BF16)
            heads[i] = mm(probs_ref[i], v)[:, :here].astype(BF16)
        for r in range(groups):
            fold(sent_refs[r], heads[pl.ds(seq ^ r, 1)][0])

    return kernel


def head_stacks(qkv_ref, image, wide, heads_here):
    masks = head_masks(wide, heads_here)
    stacks = []
    for j in (1, 2):
        rows = qkv_ref[image, :, j * wide : (j + 1) * wide]
        stacks.append(jnp.concatenate([jnp.where(m, rows, jnp.zeros_like(rows)) for m in masks]))
    return qkv_ref[image, :ROWS, :wide], stacks[0], stacks[1]


def fold(ref, rows):
    top, width = ref.shape[0], rows.shape[1]
    ref[:, :width] = rows[:top]
    ref[: rows.shape[0] - top, width:] = rows[top:]


def unfold(ref, part, count):
    width = ref.shape[1] // 2
    if part == 0:
        return ref[:, :width]
    return ref[: count - ref.shape[0], width:]


def head_rows(seq, r, here):
    return pl.ds(pl.multiple_of((seq ^ r) * here, here), here)


def route_forward(groups, here, half):
    def kernel(*refs):
        sent_refs = refs[:groups]
        cot_refs = refs[groups : 2 * groups]
        mine_ref, rows_ref, router_ref, mask_ref, counts_ref = refs[2 * groups : 2 * groups + 5]
        half_refs = refs[2 * groups + 5 : -8]
        slots_ref, resid_ref, mixed_ref, logits_ref, mix_ref, grad_ref, heads_ref, cot = refs[-8:]
        seq = lax.axis_index("seq")
        for j in range(2):
            lanes = pl.ds(pl.multiple_of(((seq & 1) ^ j) * half, 128), half)
            mix_ref[:, lanes] = half_refs[j][...]
        for r in range(groups):
            heads_ref[r, :FOLD] = unfold(sent_refs[r], 0, ROWS)
            heads_ref[r, FOLD:] = unfold(sent_refs[r], 1, ROWS)
            shard = cot_refs[r].shape[0]
            cot[pl.ds(pl.multiple_of((seq ^ r) * shard, shard), shard), :] = cot_refs[r][...]
        resid = mine_ref[...].astype(F32) + rows_ref[2:3]
        for r in range(groups):
            resid = resid + mm(heads_ref[r], mix_ref[head_rows(seq, r, here), :])
        resid_ref[...] = resid
        normed, _ = unit(resid)
        mixed = (normed * rows_ref[3:4] + rows_ref[4:5]).astype(BF16)
        mixed_ref[...] = mixed
        logits = mm(mixed, router_ref[...])
        logits_ref[...] = logits
        length = image_length(mask_ref, counts_ref, seq)
        valid = lax.broadcasted_iota(jnp.int32, (ROWS, 1), 0) < length
        dispatch = token_softmax(logits, valid)
        combine = slot_softmax(logits)
        grad = cot[:ROWS, :]
        grad = jnp.where(valid, grad, jnp.zeros_like(grad))
        grad_ref[...] = grad
        slots_ref[:, 0, :] = mm_tn(dispatch.astype(BF16), mixed).astype(BF16)
        slots_ref[:, 1, :] = mm_tn(combine.astype(BF16), grad).astype(BF16)

    return kernel


def token_softmax(logits, valid):
    masked = jnp.where(valid, logits, NEG)
    top = jnp.exp(masked - jnp.max(masked, axis=0, keepdims=True))
    return top / jnp.sum(top, axis=0, keepdims=True)


def slot_softmax(logits):
    top = jnp.exp(logits - jnp.max(logits, axis=-1, keepdims=True))
    return top / jnp.sum(top, axis=-1, keepdims=True)


def expert_values(
    x_ref, win_ref, bias_ref, wout_ref, obias_ref, back_ref, hid_ref, pre_ref, hb_ref, ob_ref
):
    x = x_ref[:, 0, :]
    g = x_ref[:, 1, :]
    ob_ref[...] = jnp.sum(g.astype(F32), axis=0, keepdims=True)
    pre = mm(x, win_ref[0]) + bias_ref[...].astype(F32)
    phi = 0.5 * (1.0 + lax.erf(pre * 2.0 ** (-0.5)))
    hidden = (pre * phi).astype(BF16)
    hid_ref[...] = hidden
    back_ref[:, 0, :] = (mm(hidden, wout_ref[0]) + obias_ref[...].astype(F32)).astype(BF16)
    slope = phi + pre * jnp.exp(-0.5 * pre * pre) * (2.0 * math.pi) ** (-0.5)
    grad_pre = (mm_nt(g, wout_ref[0]) * slope).astype(BF16)
    pre_ref[...] = grad_pre
    hb_ref[...] = jnp.sum(grad_pre.astype(F32), axis=0, keepdims=True)
    back_ref[:, 1, :] = mm_nt(grad_pre, win_ref[0]).astype(BF16)


def expert_weights(x_ref, hid_ref, pre_ref, *refs):
    gin_ref, gout_ref = refs[-2:]
    gin_ref[0] = mm_tn(x_ref[:, 0, :], pre_ref[...])
    gout_ref[0] = mm_tn(hid_ref[...], x_ref[:, 1, :])


def route_backward(groups, here, misc_w, experts):
    def kernel(*refs):
        (back_ref, resid_ref, mixed_ref, logits_ref, grad_ref, mix_ref, router_ref, rows_ref) = (
            refs[:8]
        )
        mask_ref, counts_ref = refs[8:10]
        heads_ref = refs[10]
        rest = refs[11:]
        gheads_refs = rest[:groups]
        tok, keep_ref, send_ref, misc_ref, full, turn = rest[groups:]
        seq = lax.axis_index("seq")
        length = image_length(mask_ref, counts_ref, seq)
        valid = lax.broadcasted_iota(jnp.int32, (ROWS, 1), 0) < length
        logits = logits_ref[...]
        dispatch = token_softmax(logits, valid)
        combine = slot_softmax(logits)
        resid = resid_ref[...]
        mixed = mixed_ref[...]
        slot_out = back_ref[:, 0, :]
        grad_slot = back_ref[:, 1, :]
        grad = grad_ref[...]
        out = jnp.where(valid, resid + mm(combine.astype(BF16), slot_out), 0.0).astype(BF16)
        grad_combine = mm_nt(grad, slot_out)
        grad_dispatch = mm_nt(mixed, grad_slot)
        grad_logits = combine * (
            grad_combine - jnp.sum(combine * grad_combine, axis=-1, keepdims=True)
        ) + dispatch * (grad_dispatch - jnp.sum(dispatch * grad_dispatch, axis=0, keepdims=True))
        low = grad_logits.astype(BF16)
        grad_mixed = mm(dispatch.astype(BF16), grad_slot) + mm_nt(low, router_ref[...])
        normed, root = unit(resid)
        turn[...] = jnp.zeros_like(turn)
        turn[experts + 3 : experts + 4, :] = jnp.sum(grad_mixed * normed, axis=0, keepdims=True)
        turn[experts + 4 : experts + 5, :] = jnp.sum(grad_mixed, axis=0, keepdims=True)
        grad_resid = grad.astype(F32) + unit_back(grad_mixed * rows_ref[3:4], normed, root)
        turn[experts + 2 : experts + 3, :] = jnp.sum(grad_resid, axis=0, keepdims=True)
        turn[:experts, :] = mm_tn(low, mixed)
        misc_ref[...] = turn[...]
        gr = grad_resid.astype(BF16)
        tok[...] = jnp.zeros_like(tok)
        tok[0, :ROWS, :] = out
        tok[1, :ROWS, :] = gr
        for r in range(groups):
            fold(gheads_refs[r], mm_nt(gr, mix_ref[head_rows(seq, r, here), :]).astype(BF16))
            full[head_rows(seq, r, here), :] = mm_tn(heads_ref[r], gr).astype(BF16)
        for core in range(2):

            @pl.when((seq & 1) == core)
            def _():
                for j in range(groups // 2):
                    lanes = slice(j * here, (j + 1) * here)
                    lo = (2 * j + core) * here
                    keep_ref[:, lanes] = full[:, lo : lo + here]
                    lo = (2 * j + 1 - core) * here
                    send_ref[:, lanes] = full[:, lo : lo + here]

    return kernel


def add_shares(keep_ref, got_ref, mine_ref, send_ref):
    chip = lax.axis_index("seq") // 2
    size = mine_ref.shape[1]
    for j in range(2):

        @pl.when(chip == j)
        def _():
            own, other = (slice(to * size, (to + 1) * size) for to in (j, 1 - j))
            mine_ref[...] = (keep_ref[:, own].astype(F32) + got_ref[:, own].astype(F32)).astype(BF16)
            fold(
                send_ref,
                (keep_ref[:, other].astype(F32) + got_ref[:, other].astype(F32)).astype(BF16),
            )


def attend_backward(groups, here, wide, experts):
    heads_here = HEADS // groups

    def kernel(*refs):
        gheads_refs = refs[:groups]
        qkv_ref, probs_ref, unit_ref, wpad_ref, misc_ref, token_ref = refs[groups : groups + 6]
        gqkv, keep_ref, send_ref, turn, gh, gxs, gs = refs[groups + 6 :]
        images, _, features = unit_ref.shape
        seq = lax.axis_index("seq")
        masks = head_masks(wide, heads_here)
        keys = qkv_ref.shape[1]
        scaling = HEAD_DIM ** (-0.5)
        gh[...] = jnp.zeros_like(gh)
        for r in range(groups):
            gh[pl.ds(seq ^ r, 1), :FOLD, :here] = unfold(gheads_refs[r], 0, ROWS)[None]
            gh[pl.ds(seq ^ r, 1), FOLD:, :here] = unfold(gheads_refs[r], 1, ROWS)[None]

        def by_head(stacked):
            picked = stacked[(heads_here - 1) * keys : (heads_here - 1) * keys + ROWS]
            for h in range(heads_here - 1):
                picked = jnp.where(masks[h], stacked[h * keys : h * keys + ROWS], picked)
            return picked

        for i in range(images):
            q, k, v = head_stacks(qkv_ref, i, wide, heads_here)
            go = gh[i]
            gp = mm_nt(go, v)
            for h in range(heads_here):
                lanes = slice(h * keys, (h + 1) * keys)
                probs = probs_ref[i, :, lanes].astype(F32)
                inner = jnp.sum(probs * gp[:, lanes], axis=-1, keepdims=True)
                gs[:, lanes] = (probs * (gp[:, lanes] - inner)).astype(BF16)
            rows = slice(i * ROWS, (i + 1) * ROWS)
            gqkv[rows, :wide] = (mm(gs[...], k) * scaling).astype(BF16)
            gqkv[rows, wide : 2 * wide] = (by_head(mm_tn(gs[...], q)) * scaling).astype(BF16)
            gqkv[rows, 2 * wide :] = by_head(mm_tn(probs_ref[i], go)).astype(BF16)
        gx = mm_nt(gqkv[...], wpad_ref[...])
        shard = keep_ref.shape[2]
        gxs[:, :ROWS, :] = gx.astype(BF16).reshape(images, ROWS, features)
        gxs[:, ROWS:, :] = jnp.zeros((images, gxs.shape[1] - ROWS, features), BF16)
        for j in range(2):
            for to, ref in ((seq ^ (2 * j), keep_ref), (seq ^ (2 * j + 1), send_ref)):
                rows = pl.ds(pl.multiple_of(to * shard, shard), shard)
                ref[j, :images] = gxs[:, rows, :]
                ref[j, images:] = token_ref[:, rows, :]
        normed = unit_ref[...].reshape(images * ROWS, features).astype(F32)
        turn[...] = misc_ref[...]
        turn[experts : experts + 1, :] = jnp.sum(gx * normed, axis=0, keepdims=True)
        turn[experts + 1 : experts + 2, :] = jnp.sum(gx, axis=0, keepdims=True)

    return kernel


def project_backward(pieces, here, wide, misc_w):
    def kernel(*refs):
        gqkv_ref, xa_ref, misc_ref, gmix_ref, other_ref = refs[:5]
        out_refs = refs[5 : 5 + pieces]
        full = refs[5 + pieces]
        images, _, features = xa_ref.shape
        flat = xa_ref[...].reshape(images * ROWS, features)
        gw = mm_tn(flat, gqkv_ref[...]).astype(BF16)
        for j in range(3):
            full[:, j * here : (j + 1) * here] = gw[:, j * wide : j * wide + here]
        full[:, 3 * here : 3 * here + misc_w] = misc_ref[...].T.astype(BF16)
        middle = other_ref.shape[0]
        for part, rows in ((0, slice(0, middle)), (1, slice(middle, features))):
            other = unfold(other_ref, part, features)
            gmix = gmix_ref[rows, :].astype(F32) + other.astype(F32)
            full[rows, 3 * here + misc_w :] = gmix.astype(BF16)
        if pieces == 1:
            out_refs[0][...] = full[...]
        else:
            dp = lax.axis_index("dp")
            part = out_refs[0].shape[0]
            half = part // 2

            def block(step, lo, rows):
                at = pl.multiple_of((dp ^ step) * part + lo, half)
                return full[pl.ds(at, rows), :]

            for ref, step in zip(out_refs, (0, 1, 2, 4)):
                ref[...] = block(step, 0, part)
            for ref, step, lo in ((out_refs[4], 5, 0), (out_refs[5], 6, half)):
                ref[:part, :] = block(step, 0, part)
                ref[part:, :] = block(3, lo, half)
            out_refs[6][...] = block(7, 0, half)
            out_refs[7][...] = block(7, half, half)

    return kernel


def token_backward(keep_ref, core_ref, chip_ref, tok_ref, rows_ref, out_ref, grad_ref, resid):
    seq = lax.axis_index("seq")
    images, shard, features = tok_ref.shape
    total = keep_ref[0, :images].astype(F32) + core_ref[0, :images].astype(F32)
    total = (total + chip_ref[:images].astype(F32)).reshape(images * shard, features)
    for r, got in enumerate(
        (keep_ref.at[0, images:], core_ref.at[0, images:], chip_ref.at[images : images + 2],
         chip_ref.at[images + 2 :])
    ):
        out_ref[pl.ds(seq ^ r, 1)] = got[0:1]
        resid[pl.ds(seq ^ r, 1)] = got[1:2]
    normed, root = unit(tok_ref[...].astype(F32).reshape(images * shard, features))
    back = unit_back(total * rows_ref[0:1], normed, root).reshape(images, shard, features)
    grad_ref[...] = (resid[...].astype(F32) + back).astype(BF16)


def plus(a, b):
    return (a.astype(F32) + b.astype(F32)).astype(BF16)


def reduce_last(y_ref, z_ref, first_ref, second_ref, to_y, to_z):
    half = first_ref.shape[0]
    to_y[...] = y_ref[...]
    to_z[...] = z_ref[...]
    to_y[half : 2 * half, :] = plus(y_ref[half : 2 * half, :], second_ref[...])
    to_z[:half, :] = plus(z_ref[:half, :], first_ref[...])


def reduce_blocks(beside_ref, across_ref, far_ref, y_ref, z_ref, beside, across, far):
    part = far_ref.shape[0]
    half = part // 2
    total = far_ref[...].astype(F32) + y_ref[:part, :].astype(F32)
    far[...] = (total + z_ref[:part, :].astype(F32)).astype(BF16)
    across[:half, :] = plus(across_ref[:half, :], y_ref[part:, :])
    across[half:, :] = across_ref[half:, :]
    beside[:half, :] = beside_ref[:half, :]
    beside[half:, :] = plus(beside_ref[half:, :], z_ref[part:, :])


def add_second(keep_ref, got_ref, out_ref):
    images = keep_ref.shape[1] - 2
    out_ref[:images] = (
        keep_ref[1, :images].astype(F32) + got_ref[1, :images].astype(F32)
    ).astype(BF16)
    out_ref[images : images + 2] = keep_ref[1, images:]
    out_ref[images + 2 :] = got_ref[1, images:]


def sum_parts(*refs):
    total = refs[0][...].astype(F32)
    for ref in refs[1:-1]:
        total = total + ref[...].astype(F32)
    refs[-1][...] = total.astype(BF16)


def spread_parts(groups, here, misc_w, experts):
    def kernel(*refs):
        in_refs = refs[:groups]
        qkv_ref, mix_ref, router_ref = refs[groups : groups + 3]
        row_refs = refs[groups + 3 :]
        features = mix_ref.shape[1]
        seq = lax.axis_index("seq")
        for s in range(groups):

            @pl.when(seq == s)
            def _():
                for r in range(groups):
                    g = s ^ r
                    for j in range(3):
                        lo = j * features + g * here
                        part = in_refs[r][:, j * here : (j + 1) * here]
                        qkv_ref[:, lo : lo + here] = part.astype(F32)
                    part = in_refs[r][:, 3 * here + misc_w :]
                    mix_ref[:, g * here : (g + 1) * here] = part.astype(F32)

        misc = in_refs[0][:, 3 * here : 3 * here + misc_w].astype(F32)
        for r in range(1, groups):
            misc = misc + in_refs[r][:, 3 * here : 3 * here + misc_w].astype(F32)
        misc = misc.T
        router_ref[...] = misc[:experts]
        for j in range(5):
            row_refs[j][...] = misc[experts + j : experts + j + 1]

    return kernel


def body(
    tokens,
    pad_mask,
    counts,
    attn_gain,
    attn_shift,
    qkv_weight,
    mix_weight,
    mix_bias,
    moe_gain,
    moe_shift,
    router,
    expert_in,
    hidden_bias,
    expert_out,
    output_bias,
    cotangent,
):
    images, shard, features = tokens.shape
    groups = lax.axis_size("seq")
    lanes = lax.axis_size("dp")
    devices = groups * lanes
    part = mix_weight.shape[0]
    experts = router.shape[1]
    hidden = expert_in.shape[2]
    misc_w = -(-(experts + 8) // 64) * 64
    here = HEADS // groups * HEAD_DIM
    wide = -(-here // 128) * 128
    half = features // 2
    full = groups * shard
    direct = lanes == 8 and part % 32 == 0
    piece_w = 3 * here + misc_w + here

    def swap(a, axis, step):
        return lax.ppermute(a, axis, [(i, i ^ step) for i in range(lax.axis_size(axis))])

    def exchange(parts):
        moved = {r: swap(parts[r], "seq", r) for r in range(groups - 1, 0, -1)}
        return [parts[0]] + [moved[r] for r in range(1, groups)]

    packed_w = 3 * here + misc_w + half
    piece, *cots = kernel_call(
        pack_inputs(groups, here, half, misc_w, experts),
        [qkv_weight, router.T]
        + [v.reshape(1, part) for v in (attn_gain, attn_shift, mix_bias, moe_gain, moe_shift)]
        + [mix_weight, cotangent],
        [((part, packed_w), BF16)] + [((shard, features), BF16)] * groups,
        [pltpu.VMEM((misc_w, -(-part // 128) * 128), F32)],
        limit=ALL_VMEM,
        hbm_in=tuple(range(9)),
    )
    cots = exchange(cots)
    over = swap(tokens, "seq", 2)
    near = swap(tokens, "seq", 1)
    if direct:
        far, across, beside = (swap(piece, "dp", step) for step in (4, 2, 1))
        far, across, beside, over, cots[2] = lax.optimization_barrier(
            (far, across, beside, over, cots[2])
        )
        longer = ((part + part // 2, packed_w), BF16)
        to_y, to_z = kernel_call(forward_blocks, [beside, across, far], [longer] * 2, limit=4)
        by_y, by_z = swap(to_y, "dp", 1), swap(to_z, "dp", 2)
        by_y, by_z, near, cots[1], cots[3] = lax.optimization_barrier(
            (by_y, by_z, near, cots[1], cots[3])
        )
        a, b = kernel_call(forward_last, [by_y, by_z], [((part // 2, packed_w), BF16)] * 2, limit=4)
        piece_parts = [piece, beside, across, far, by_y, by_z, swap(a, "dp", 1), swap(b, "dp", 2)]
    else:
        piece_parts = [lax.all_gather(piece, "dp", axis=0, tiled=True)]
    normed, units, mine = kernel_call(
        normalize_tokens(groups),
        [tokens, near, over, swap(over, "seq", 1)],
        [
            ((images, ROWS, features), F32),
            ((images, ROWS, features), BF16),
            ((ROWS, features), BF16),
        ],
        [pltpu.VMEM((images, full, features), BF16)],
        limit=8,
        flops=1e8,
    )
    outs = kernel_call(
        attend_forward(groups, len(piece_parts), here, wide, misc_w, experts),
        [normed, pad_mask, counts] + piece_parts,
        [((FOLD, 2 * here), BF16)] * groups
        + [
            ((features, half), BF16),
            ((images, ROWS, HEADS // groups * full), BF16),
            ((images, ROWS, features), BF16),
            ((images, full, 3 * wide), BF16),
            ((features, 3 * wide), BF16),
            ((8, features), F32),
            ((features, experts), BF16),
        ],
        [
            pltpu.VMEM((features, packed_w), BF16),
            pltpu.VMEM((images, ROWS, here), BF16),
        ],
        smem=(2,),
        limit=16,
        flops=1e8,
    )
    sent = exchange(outs[:groups])
    mix_half, probs, xa, qkv, wpad, rows, router_full = outs[groups:]
    slots, resid, mixed, logits, mix_full, grad, heads = kernel_call(
        route_forward(groups, here, half),
        sent
        + cots
        + [mine, rows, router_full, pad_mask, counts, mix_half, swap(mix_half, "seq", 1)],
        [
            ((experts, 2, features), BF16),
            ((ROWS, features), F32),
            ((ROWS, features), BF16),
            ((ROWS, experts), F32),
            ((features, features), BF16),
            ((ROWS, features), BF16),
            ((groups, ROWS, here), BF16),
        ],
        [pltpu.VMEM((full, features), BF16)],
        smem=(2 * groups + 4,),
        limit=10,
        flops=5e9,
    )
    slots = lax.all_to_all(slots, ("dp", "seq"), split_axis=0, concat_axis=0, tiled=True)
    block = min(512, hidden)
    back, hid, grad_pre, grad_hidden_bias, grad_output_bias = kernel_call(
        expert_values,
        [slots, expert_in, hidden_bias, expert_out, output_bias],
        [
            ((devices, 2, features), BF16),
            ((devices, hidden), BF16),
            ((devices, hidden), BF16),
            ((1, hidden), F32),
            ((1, features), F32),
        ],
        limit=8,
        flops=5e9,
    )
    back = lax.all_to_all(back, ("dp", "seq"), split_axis=0, concat_axis=0, tiled=True)

    def expert_gradients(first, count, ins):
        lane_spec = pl.BlockSpec((devices, block), lambda i: (0, i + first))
        return pl.pallas_call(
            expert_weights,
            grid=(count,),
            in_specs=[pl.BlockSpec((devices, 2, features), lambda i: (0, 0, 0))]
            + [lane_spec] * 2
            + [pl.BlockSpec(memory_space=pl.ANY)] * (len(ins) - 3),
            out_specs=[
                pl.BlockSpec((1, features, block), lambda i: (0, 0, i + first)),
                pl.BlockSpec((1, block, features), lambda i: (0, i + first, 0)),
            ],
            out_shape=[
                jax.ShapeDtypeStruct((1, features, hidden), F32),
                jax.ShapeDtypeStruct((1, hidden, features), F32),
            ],
            input_output_aliases={i: i - 3 for i in range(3, len(ins))},
            compiler_params=pltpu.CompilerParams(vmem_limit_bytes=12 * 2**20),
            cost_estimate=pl.CostEstimate(
                flops=1 if first else 10**11, bytes_accessed=0, transcendentals=0
            ),
        )(*ins)

    steps = hidden // block
    early = steps // 3
    expert_grads = expert_gradients(0, early, [slots, hid, grad_pre])
    outs = kernel_call(
        route_backward(groups, here, misc_w, experts),
        [back, resid, mixed, logits, grad, mix_full, router_full, rows, pad_mask, counts, heads],
        [((FOLD, 2 * here), BF16)] * groups
        + [((2, full, features), BF16)]
        + [((features, groups // 2 * here), BF16)] * 2
        + [((misc_w, features), F32)],
        [pltpu.VMEM((features, features), BF16), pltpu.VMEM((misc_w, features), F32)],
        smem=(9,),
        limit=16,
        flops=5e9,
    )
    gheads = exchange(outs[:groups])
    token_rows, keep, send, misc = outs[groups:]
    gmix, gmix_send = kernel_call(
        add_shares,
        [keep, swap(send, "seq", 1)],
        [((features, here), BF16), ((features // 2, 2 * here), BF16)],
        limit=8,
    )
    gmix, gmix_send, own = lax.optimization_barrier((gmix, gmix_send, gheads[0]))
    gmix_other = swap(gmix_send, "seq", 2)
    gqkv, gx, gx_send, misc = kernel_call(
        attend_backward(groups, here, wide, experts),
        [own] + gheads[1:] + [qkv, probs, units, wpad, misc, token_rows],
        [
            ((images * ROWS, 3 * wide), BF16),
            ((2, images + 2, shard, features), BF16),
            ((2, images + 2, shard, features), BF16),
            ((misc_w, features), F32),
        ],
        [
            pltpu.VMEM((images, ROWS, wide), BF16),
            pltpu.VMEM((images, full, features), BF16),
            pltpu.VMEM((ROWS, HEADS // groups * full), BF16),
        ],
        limit=16,
        flops=1e10,
    )
    gx_core = swap(gx_send, "seq", 1)
    whole = ((part, piece_w), BF16)
    longer = ((part + part // 2, piece_w), BF16)
    shorter = ((part // 2, piece_w), BF16)
    out_parts = [whole] * 4 + [longer] * 2 + [shorter] * 2
    if not direct:
        out_parts = [((features, piece_w), BF16)]
    outs = kernel_call(
        project_backward(len(out_parts), here, wide, misc_w),
        [gqkv, xa, misc, gmix, gmix_other],
        out_parts,
        [pltpu.VMEM((features, piece_w), BF16)],
        limit=16,
        flops=2e10,
    )
    gx_core, _ = lax.optimization_barrier((gx_core, outs[0]))
    if direct:
        own, beside, across, far, to_y, to_z, first, second = outs
        first, second = swap(first, "dp", 1), swap(second, "dp", 2)
        first, second, *expert_grads = lax.optimization_barrier([first, second] + list(expert_grads))
        expert_grads = expert_gradients(early, steps - early, [slots, hid, grad_pre, *expert_grads])
        to_y, to_z = kernel_call(
            reduce_last, [to_y, to_z, first, second], [longer] * 2, limit=4
        )
        by_y, by_z = swap(to_y, "dp", 1), swap(to_z, "dp", 2)
        by_y, by_z, *expert_grads = lax.optimization_barrier([by_y, by_z] + list(expert_grads))
        beside, across, far = kernel_call(
            reduce_blocks, [beside, across, far, by_y, by_z], [whole] * 3, limit=4
        )
        sums = [swap(far, "dp", 4), swap(across, "dp", 2), swap(beside, "dp", 1), own]
    else:
        expert_grads = expert_gradients(early, steps - early, [slots, hid, grad_pre, *expert_grads])
        arrived = lax.all_to_all(outs[0], "dp", split_axis=0, concat_axis=0, tiled=True)
        sums = [arrived[r * part : (r + 1) * part] for r in range(lanes)]
    (gx_sum,) = kernel_call(
        add_second, [gx, gx_core], [((images + 4, shard, features), BF16)], limit=4
    )
    gx_chip = swap(gx_sum, "seq", 2)
    (share,) = kernel_call(sum_parts, sums, [whole], limit=4)
    share, gx_chip = lax.optimization_barrier((share, gx_chip))
    block_out, input_grad = kernel_call(
        token_backward,
        [gx, gx_core, gx_chip, tokens, rows],
        [((images, shard, features), BF16), ((images, shard, features), BF16)],
        [pltpu.VMEM((images, shard, features), BF16)],
        limit=8,
        flops=2e9,
    )
    share_over = swap(share, "seq", 2)
    shares = [share, swap(share, "seq", 1), share_over, swap(share_over, "seq", 1)]
    grad_qkv, grad_mix, grad_router, *vector_rows = kernel_call(
        spread_parts(groups, here, misc_w, experts),
        shares,
        [((part, 3 * features), F32), ((part, features), F32), ((experts, part), F32)]
        + [((1, part), F32)] * 5,
        limit=8,
    )
    vector_rows = [v.reshape(part) for v in vector_rows]
    return (
        block_out,
        input_grad,
        vector_rows[0],
        vector_rows[1],
        grad_qkv,
        grad_mix,
        vector_rows[2],
        vector_rows[3],
        vector_rows[4],
        grad_router.T,
        expert_grads[0],
        grad_hidden_bias,
        expert_grads[1],
        grad_output_bias,
    )


def solution(mesh):
    return jax.shard_map(
        body,
        mesh=mesh,
        in_specs=(
            P("dp", "seq", None),
            P("dp", None),
            P("dp"),
            P("dp"),
            P("dp"),
            P("dp", None),
            P("dp", None),
            P("dp"),
            P("dp"),
            P("dp"),
            P("dp", None),
            P(("dp", "seq"), None, None),
            P(("dp", "seq"), None),
            P(("dp", "seq"), None, None),
            P(("dp", "seq"), None),
            P("dp", "seq", None),
        ),
        out_specs=(
            P("dp", "seq", None),
            P("dp", "seq", None),
            P("dp"),
            P("dp"),
            P("dp", None),
            P("dp", None),
            P("dp"),
            P("dp"),
            P("dp"),
            P("dp", None),
            P(("dp", "seq"), None, None),
            P(("dp", "seq"), None),
            P(("dp", "seq"), None, None),
            P(("dp", "seq"), None),
        ),
        check_vma=False,
    )
```

```python
import math

import jax
import jax.numpy as jnp
from jax import lax
from jax.experimental import pallas as pl
from jax.experimental.pallas import tpu as pltpu
from jax.sharding import PartitionSpec as P

HEADS = 12
HEAD_DIM = 64
EPS = 1e-06
NEG = -1000000000.0
BF16 = jnp.bfloat16
F32 = jnp.float32
ALL_VMEM = 62.6
FOLD = 112
ROWS = 208
NT = (((1,), (1,)), ((), ()))
TN = (((0,), (0,)), ((), ()))


def mm(a, b):
    return jnp.dot(a, b, preferred_element_type=F32)


def mm_nt(a, b):
    return lax.dot_general(a, b, NT, preferred_element_type=F32)


def mm_tn(a, b):
    return lax.dot_general(a, b, TN, preferred_element_type=F32)


def unit(values):
    center = values - jnp.mean(values, axis=-1, keepdims=True)
    spread = jnp.mean(center * center, axis=-1, keepdims=True)
    root = lax.rsqrt(spread + EPS)
    return center * root, root


def unit_back(scaled, rows, root):
    inner = jnp.mean(scaled * rows, axis=-1, keepdims=True)
    return root * (scaled - jnp.mean(scaled, axis=-1, keepdims=True) - rows * inner)


def lane_mask(index, width):
    lane = lax.broadcasted_iota(jnp.int32, (1, width), 1)
    return (lane >= index * HEAD_DIM) & (lane < (index + 1) * HEAD_DIM)


def image_length(mask_ref, counts_ref, image):
    which = lax.broadcasted_iota(jnp.int32, mask_ref.shape, 0)
    real = jnp.where(which == image, mask_ref[...], 0)
    total = jnp.sum(jnp.sum(real, axis=1, keepdims=True), axis=0, keepdims=True)
    return jnp.where(image < counts_ref[0], total, 0)


def kernel_call(
    kernel, ins, outs, scratch=(), limit=48, smem=(), hbm_in=(), hbm_out=(), aliases=None, flops=1
):
    kw = {
        "input_output_aliases": aliases or {},
        "cost_estimate": pl.CostEstimate(flops=int(flops), bytes_accessed=0, transcendentals=0),
    }
    n_in, n_out, n_own = len(ins), len(outs), len(scratch)
    n_staged = len(hbm_in) + len(hbm_out)

    def wrapped(*refs):
        in_refs = list(refs[:n_in])
        out_refs = list(refs[n_in : n_in + n_out])
        own = refs[n_in + n_out : n_in + n_out + n_own]
        stages = refs[n_in + n_out + n_own :]
        reads, writes = [], {}
        for j, i in enumerate(hbm_in):
            reads.append(pltpu.make_async_copy(in_refs[i], stages[j], stages[-1].at[j]))
            in_refs[i] = stages[j]
        for j, i in enumerate(hbm_out, len(hbm_in)):
            writes[i] = pltpu.make_async_copy(stages[j], out_refs[i], stages[-1].at[j])
            out_refs[i] = stages[j]
        for copy in reads:
            copy.start()
        for copy in reads:
            copy.wait()
        kernel(*in_refs, *out_refs, *own)
        for copy in writes.values():
            copy.start()
        for copy in writes.values():
            copy.wait()

    def spec(i, staged):
        if i in staged:
            return pl.BlockSpec(memory_space=pltpu.HBM)
        return pl.BlockSpec(memory_space=pltpu.VMEM)

    in_specs = [
        pl.BlockSpec(memory_space=pltpu.SMEM) if i in smem else spec(i, hbm_in)
        for i in range(n_in)
    ]
    scratch = list(scratch)
    scratch += [pltpu.VMEM(ins[i].shape, ins[i].dtype) for i in hbm_in]
    scratch += [pltpu.VMEM(*outs[i]) for i in hbm_out]
    if n_staged:
        scratch.append(pltpu.SemaphoreType.DMA((n_staged,)))
    call = pl.pallas_call(
        wrapped,
        in_specs=in_specs,
        out_specs=[spec(i, hbm_out) for i in range(n_out)],
        out_shape=[jax.ShapeDtypeStruct(shape, kind) for shape, kind in outs],
        scratch_shapes=scratch,
        compiler_params=pltpu.CompilerParams(vmem_limit_bytes=int(limit * 2**20)),
        **kw,
    )
    return list(call(*ins))


def place(full, refs, dp):
    if len(refs) == 1:
        full[...] = refs[0][...]
        return
    part = refs[0].shape[0]
    half = part // 2

    def put(ref, rows, step, lo):
        at = pl.multiple_of((dp ^ step) * part + lo, half)
        full[pl.ds(at, rows.stop - rows.start), :] = ref[rows, :]

    whole, rest = slice(0, part), slice(part, part + half)
    for ref, step in zip(refs, (0, 1, 2, 4, 5, 6)):
        put(ref, whole, step, 0)
    put(refs[4], rest, 3, 0)
    put(refs[5], rest, 3, half)
    put(refs[6], slice(0, half), 7, 0)
    put(refs[7], slice(0, half), 7, half)


def forward_blocks(beside, across, far, y_ref, z_ref):
    part = far.shape[0]
    half = part // 2
    y_ref[:part, :] = far[...]
    y_ref[part:, :] = across[:half, :]
    z_ref[:part, :] = far[...]
    z_ref[part:, :] = beside[half:, :]


def forward_last(y_ref, z_ref, first_ref, second_ref):
    half = first_ref.shape[0]
    first_ref[...] = z_ref[:half, :]
    second_ref[...] = y_ref[half : 2 * half, :]


def head_masks(width, heads_here):
    return [lane_mask(h, width) for h in range(heads_here)]


def pack_inputs(groups, here, half, misc_w, experts):
    def kernel(*refs):
        qkv_ref, router_ref = refs[:2]
        vectors = refs[2:7]
        mix_ref, piece_ref, turn = refs[7:]
        seq = lax.axis_index("seq")
        features = qkv_ref.shape[1] // 3
        part = qkv_ref.shape[0]
        for g in range(groups):

            @pl.when(seq == g)
            def _():
                for j in range(3):
                    lo = j * features + g * here
                    piece_ref[:, j * here : (j + 1) * here] = qkv_ref[:, lo : lo + here]

        turn[...] = jnp.zeros_like(turn)
        turn[:experts, :part] = router_ref[...].astype(F32)
        for j in range(5):
            turn[experts + j : experts + j + 1, :part] = vectors[j][...].astype(F32)
        lo = 3 * here + misc_w
        piece_ref[:, 3 * here : lo] = turn[...].T[:part].astype(BF16)
        piece_ref[:, lo:] = mix_ref[:, pl.ds(pl.multiple_of((seq & 1) * half, 128), half)]

    return kernel


def by_image_owner(cot_ref, *cot_refs):
    seq = lax.axis_index("seq")
    for r in range(len(cot_refs)):
        cot_refs[r][...] = cot_ref[pl.ds(seq ^ r, 1)][0]


def normalize_tokens(groups):
    def kernel(*refs):
        tok_refs = refs[:groups]
        normed_ref, unit_ref, mine_ref, tok = refs[groups:]
        seq = lax.axis_index("seq")
        images, shard, _ = tok_refs[0].shape
        for r in range(groups):
            rows = pl.ds(pl.multiple_of((seq ^ r) * shard, shard), shard)
            tok[:, rows, :] = tok_refs[r][...]
        mine_ref[...] = tok[pl.ds(seq, 1), :ROWS, :][0]
        for i in range(images):
            normed, _ = unit(tok[i, :ROWS, :].astype(F32))
            normed_ref[i] = normed
            unit_ref[i] = normed.astype(BF16)

    return kernel


def attend_forward(groups, pieces, here, wide, misc_w, experts):
    heads_here = HEADS // groups

    def kernel(*refs):
        normed_ref, mask_ref, counts_ref = refs[:3]
        w_refs = refs[3 : 3 + pieces]
        sent_refs = refs[3 + pieces : 3 + pieces + groups]
        rest = refs[3 + pieces + groups :]
        (half_ref, probs_ref, xa_ref, qkv_ref, wpad_ref, rows_ref, router_ref, dense, heads) = rest
        seq = lax.axis_index("seq")
        images, _, features = normed_ref.shape
        place(dense, w_refs, lax.axis_index("dp"))
        wpad_ref[...] = jnp.zeros_like(wpad_ref)
        for j in range(3):
            wpad_ref[:, j * wide : j * wide + here] = dense[:, j * here : (j + 1) * here]
        half_ref[...] = dense[:, 3 * here + misc_w :]
        misc = dense[:, 3 * here : 3 * here + misc_w]
        router_ref[...] = misc[:, :experts]
        rows_ref[...] = misc.astype(F32).T[experts : experts + 8]
        xa_ref[...] = (normed_ref[...] * rows_ref[0:1][None] + rows_ref[1:2][None]).astype(BF16)
        flat = xa_ref[...].reshape(images * ROWS, features)
        qkv_ref[:, :ROWS, :] = (
            mm(flat, wpad_ref[...]).astype(BF16).reshape(images, ROWS, 3 * wide)
        )
        keys = qkv_ref.shape[1]
        qkv_ref[:, ROWS:, :] = jnp.zeros((images, keys - ROWS, 3 * wide), BF16)
        place_of_key = lax.broadcasted_iota(jnp.int32, (1, keys), 1)
        for i in range(images):
            valid = place_of_key < image_length(mask_ref, counts_ref, i)
            q, k, v = head_stacks(qkv_ref, i, wide, heads_here)
            scores = mm_nt(q, k) * HEAD_DIM ** (-0.5)
            for h in range(heads_here):
                lanes = slice(h * keys, (h + 1) * keys)
                masked = jnp.where(valid, scores[:, lanes], NEG)
                top = jnp.exp(masked - jnp.max(masked, axis=-1, keepdims=True))
                total = jnp.sum(top, axis=-1, keepdims=True)
                probs_ref[i, :, lanes] = (top / total).astype(BF16)
            heads[i] = mm(probs_ref[i], v)[:, :here].astype(BF16)
        for r in range(groups):
            fold(sent_refs[r], heads[pl.ds(seq ^ r, 1)][0])

    return kernel


def head_stacks(qkv_ref, image, wide, heads_here):
    masks = head_masks(wide, heads_here)
    stacks = []
    for j in (1, 2):
        rows = qkv_ref[image, :, j * wide : (j + 1) * wide]
        stacks.append(jnp.concatenate([jnp.where(m, rows, jnp.zeros_like(rows)) for m in masks]))
    return qkv_ref[image, :ROWS, :wide], stacks[0], stacks[1]


def fold(ref, rows):
    top, width = ref.shape[0], rows.shape[1]
    ref[:, :width] = rows[:top]
    ref[: rows.shape[0] - top, width:] = rows[top:]


def unfold(ref, part, count):
    width = ref.shape[1] // 2
    if part == 0:
        return ref[:, :width]
    return ref[: count - ref.shape[0], width:]


def head_rows(seq, r, here):
    return pl.ds(pl.multiple_of((seq ^ r) * here, here), here)


def route_forward(groups, here, half):
    def kernel(*refs):
        sent_refs = refs[:groups]
        cot_refs = refs[groups : 2 * groups]
        mine_ref, rows_ref, router_ref, mask_ref, counts_ref = refs[2 * groups : 2 * groups + 5]
        half_refs = refs[2 * groups + 5 : -8]
        slots_ref, resid_ref, mixed_ref, logits_ref, mix_ref, grad_ref, heads_ref, cot = refs[-8:]
        seq = lax.axis_index("seq")
        for j in range(2):
            lanes = pl.ds(pl.multiple_of(((seq & 1) ^ j) * half, 128), half)
            mix_ref[:, lanes] = half_refs[j][...]
        for r in range(groups):
            heads_ref[r, :FOLD] = unfold(sent_refs[r], 0, ROWS)
            heads_ref[r, FOLD:] = unfold(sent_refs[r], 1, ROWS)
            shard = cot_refs[r].shape[0]
            cot[pl.ds(pl.multiple_of((seq ^ r) * shard, shard), shard), :] = cot_refs[r][...]
        resid = mine_ref[...].astype(F32) + rows_ref[2:3]
        for r in range(groups):
            resid = resid + mm(heads_ref[r], mix_ref[head_rows(seq, r, here), :])
        resid_ref[...] = resid
        normed, _ = unit(resid)
        mixed = (normed * rows_ref[3:4] + rows_ref[4:5]).astype(BF16)
        mixed_ref[...] = mixed
        logits = mm(mixed, router_ref[...])
        logits_ref[...] = logits
        length = image_length(mask_ref, counts_ref, seq)
        valid = lax.broadcasted_iota(jnp.int32, (ROWS, 1), 0) < length
        dispatch = token_softmax(logits, valid)
        combine = slot_softmax(logits)
        grad = cot[:ROWS, :]
        grad = jnp.where(valid, grad, jnp.zeros_like(grad))
        grad_ref[...] = grad
        slots_ref[:, 0, :] = mm_tn(dispatch.astype(BF16), mixed).astype(BF16)
        slots_ref[:, 1, :] = mm_tn(combine.astype(BF16), grad).astype(BF16)

    return kernel


def token_softmax(logits, valid):
    masked = jnp.where(valid, logits, NEG)
    top = jnp.exp(masked - jnp.max(masked, axis=0, keepdims=True))
    return top / jnp.sum(top, axis=0, keepdims=True)


def slot_softmax(logits):
    top = jnp.exp(logits - jnp.max(logits, axis=-1, keepdims=True))
    return top / jnp.sum(top, axis=-1, keepdims=True)


def expert_values(
    x_ref, win_ref, bias_ref, wout_ref, obias_ref, back_ref, hid_ref, pre_ref, hb_ref, ob_ref
):
    x = x_ref[:, 0, :]
    g = x_ref[:, 1, :]
    ob_ref[...] = jnp.sum(g.astype(F32), axis=0, keepdims=True)
    pre = mm(x, win_ref[0]) + bias_ref[...].astype(F32)
    phi = 0.5 * (1.0 + lax.erf(pre * 2.0 ** (-0.5)))
    hidden = (pre * phi).astype(BF16)
    hid_ref[...] = hidden
    back_ref[:, 0, :] = (mm(hidden, wout_ref[0]) + obias_ref[...].astype(F32)).astype(BF16)
    slope = phi + pre * jnp.exp(-0.5 * pre * pre) * (2.0 * math.pi) ** (-0.5)
    grad_pre = (mm_nt(g, wout_ref[0]) * slope).astype(BF16)
    pre_ref[...] = grad_pre
    hb_ref[...] = jnp.sum(grad_pre.astype(F32), axis=0, keepdims=True)
    back_ref[:, 1, :] = mm_nt(grad_pre, win_ref[0]).astype(BF16)


def expert_weights(x_ref, hid_ref, pre_ref, *refs):
    gin_ref, gout_ref = refs[-2:]
    gin_ref[0] = mm_tn(x_ref[:, 0, :], pre_ref[...])
    gout_ref[0] = mm_tn(hid_ref[...], x_ref[:, 1, :])


def route_backward(groups, here, misc_w, experts):
    def kernel(*refs):
        (back_ref, resid_ref, mixed_ref, logits_ref, grad_ref, mix_ref, router_ref, rows_ref) = (
            refs[:8]
        )
        mask_ref, counts_ref = refs[8:10]
        heads_ref = refs[10]
        rest = refs[11:]
        gheads_refs = rest[:groups]
        tok, keep_ref, send_ref, misc_ref, full, turn = rest[groups:]
        seq = lax.axis_index("seq")
        length = image_length(mask_ref, counts_ref, seq)
        valid = lax.broadcasted_iota(jnp.int32, (ROWS, 1), 0) < length
        logits = logits_ref[...]
        dispatch = token_softmax(logits, valid)
        combine = slot_softmax(logits)
        resid = resid_ref[...]
        mixed = mixed_ref[...]
        slot_out = back_ref[:, 0, :]
        grad_slot = back_ref[:, 1, :]
        grad = grad_ref[...]
        out = jnp.where(valid, resid + mm(combine.astype(BF16), slot_out), 0.0).astype(BF16)
        grad_combine = mm_nt(grad, slot_out)
        grad_dispatch = mm_nt(mixed, grad_slot)
        grad_logits = combine * (
            grad_combine - jnp.sum(combine * grad_combine, axis=-1, keepdims=True)
        ) + dispatch * (grad_dispatch - jnp.sum(dispatch * grad_dispatch, axis=0, keepdims=True))
        low = grad_logits.astype(BF16)
        grad_mixed = mm(dispatch.astype(BF16), grad_slot) + mm_nt(low, router_ref[...])
        normed, root = unit(resid)
        turn[...] = jnp.zeros_like(turn)
        turn[experts + 3 : experts + 4, :] = jnp.sum(grad_mixed * normed, axis=0, keepdims=True)
        turn[experts + 4 : experts + 5, :] = jnp.sum(grad_mixed, axis=0, keepdims=True)
        grad_resid = grad.astype(F32) + unit_back(grad_mixed * rows_ref[3:4], normed, root)
        turn[experts + 2 : experts + 3, :] = jnp.sum(grad_resid, axis=0, keepdims=True)
        turn[:experts, :] = mm_tn(low, mixed)
        misc_ref[...] = turn[...]
        gr = grad_resid.astype(BF16)
        tok[...] = jnp.zeros_like(tok)
        tok[0, :ROWS, :] = out
        tok[1, :ROWS, :] = gr
        for r in range(groups):
            fold(gheads_refs[r], mm_nt(gr, mix_ref[head_rows(seq, r, here), :]).astype(BF16))
            full[head_rows(seq, r, here), :] = mm_tn(heads_ref[r], gr).astype(BF16)
        for core in range(2):

            @pl.when((seq & 1) == core)
            def _():
                for j in range(groups // 2):
                    lanes = slice(j * here, (j + 1) * here)
                    lo = (2 * j + core) * here
                    keep_ref[:, lanes] = full[:, lo : lo + here]
                    lo = (2 * j + 1 - core) * here
                    send_ref[:, lanes] = full[:, lo : lo + here]

    return kernel


def add_shares(parts, size):
    def kernel(keep_ref, got_ref, *refs):
        mine_refs, send_refs = refs[: len(parts)], refs[len(parts) : -1]
        total = refs[-1]
        total[...] = (keep_ref[...].astype(F32) + got_ref[...].astype(F32)).astype(BF16)
        chip = lax.axis_index("seq") // 2
        dp = lax.axis_index("dp")
        width = mine_refs[0].shape[1]

        def block(step, lanes):
            if size == total.shape[0]:
                return total[:, lanes]
            return total[pl.ds(pl.multiple_of((dp ^ step) * size, size), size), lanes]

        for j in range(2):

            @pl.when(chip == j)
            def _():
                own, other = (slice(to * width, (to + 1) * width) for to in (j, 1 - j))
                for steps, mine, send in zip(parts, mine_refs, send_refs):
                    for k, step in enumerate(steps):
                        mine[k * size : (k + 1) * size, :] = block(step, own)
                    fold(send, jnp.concatenate([block(step, other) for step in steps]))

    return kernel


def both_chips(mine_ref, other_ref):
    count, half = mine_ref.shape[0], other_ref.shape[0]
    return jnp.concatenate(
        [
            mine_ref[:half, :].astype(F32) + unfold(other_ref, 0, count).astype(F32),
            mine_ref[half:, :].astype(F32) + unfold(other_ref, 1, count).astype(F32),
        ]
    )


def image_backward(gheads_ref, image, qkv_ref, probs_ref, gqkv, gh, gs, heads_here):
    keys = qkv_ref.shape[1]
    wide = gh.shape[1]
    here = gheads_ref.shape[1] // 2
    masks = head_masks(wide, heads_here)
    scaling = HEAD_DIM ** (-0.5)
    gh[:FOLD, :here] = unfold(gheads_ref, 0, ROWS)
    gh[FOLD:, :here] = unfold(gheads_ref, 1, ROWS)

    def by_head(stacked):
        picked = stacked[(heads_here - 1) * keys : (heads_here - 1) * keys + ROWS]
        for h in range(heads_here - 1):
            picked = jnp.where(masks[h], stacked[h * keys : h * keys + ROWS], picked)
        return picked

    q, k, v = head_stacks(qkv_ref, image, wide, heads_here)
    go = gh[...]
    gp = mm_nt(go, v)
    for h in range(heads_here):
        lanes = slice(h * keys, (h + 1) * keys)
        probs = probs_ref[image, :, lanes].astype(F32)
        inner = jnp.sum(probs * gp[:, lanes], axis=-1, keepdims=True)
        gs[:, lanes] = (probs * (gp[:, lanes] - inner)).astype(BF16)
    rows = pl.ds(pl.multiple_of(image * ROWS, ROWS), ROWS)
    gqkv[rows, :wide] = (mm(gs[...], k) * scaling).astype(BF16)
    gqkv[rows, wide : 2 * wide] = (by_head(mm_tn(gs[...], q)) * scaling).astype(BF16)
    gqkv[rows, 2 * wide :] = by_head(mm_tn(probs_ref[image], go)).astype(BF16)


def attend_backward_near(heads_here):
    def kernel(own_ref, near_ref, qkv_ref, probs_ref, gqkv, gh, gs):
        seq = lax.axis_index("seq")
        gh[...] = jnp.zeros_like(gh)
        for r, ref in enumerate((own_ref, near_ref)):
            image_backward(ref, seq ^ r, qkv_ref, probs_ref, gqkv, gh, gs, heads_here)

    return kernel


def attend_backward_far(groups, here, wide, misc_w, experts):
    heads_here = HEADS // groups

    def kernel(*refs):
        gheads_refs = refs[: groups - 2]
        qkv_ref, probs_ref, xa_ref, unit_ref, wpad_ref, misc_ref, token_ref = refs[
            groups - 2 : groups + 5
        ]
        gqkv, keep_ref, send_ref, gw_ref, gh, gs, gxs, turn = refs[groups + 6 :]
        images, _, features = unit_ref.shape
        seq = lax.axis_index("seq")
        gh[...] = jnp.zeros_like(gh)
        for j, ref in enumerate(gheads_refs):
            image_backward(ref, seq ^ (j + 2), qkv_ref, probs_ref, gqkv, gh, gs, heads_here)
        gx = mm_nt(gqkv[...], wpad_ref[...])
        shard = keep_ref.shape[2]
        gxs[:, :ROWS, :] = gx.astype(BF16).reshape(images, ROWS, features)
        gxs[:, ROWS:, :] = jnp.zeros((images, gxs.shape[1] - ROWS, features), BF16)
        for j in range(2):
            for to, ref in ((seq ^ (2 * j), keep_ref), (seq ^ (2 * j + 1), send_ref)):
                rows = pl.ds(pl.multiple_of(to * shard, shard), shard)
                ref[j, :images] = gxs[:, rows, :]
                ref[j, images:] = token_ref[:, rows, :]
        normed = unit_ref[...].reshape(images * ROWS, features).astype(F32)
        turn[...] = misc_ref[...]
        turn[experts : experts + 1, :] = jnp.sum(gx * normed, axis=0, keepdims=True)
        turn[experts + 1 : experts + 2, :] = jnp.sum(gx, axis=0, keepdims=True)
        gw_ref[:, 3 * here :] = turn[...].T.astype(BF16)
        gw = mm_tn(xa_ref[...].reshape(images * ROWS, features), gqkv[...]).astype(BF16)
        for j in range(3):
            gw_ref[:, j * here : (j + 1) * here] = gw[:, j * wide : j * wide + here]

    return kernel


def cut_gradients(gw_ref, mine_ref, other_ref, *out_refs):
    width = gw_ref.shape[1]
    gmix = both_chips(mine_ref, other_ref).astype(BF16)
    if len(out_refs) == 1:
        out_refs[0][:, :width] = gw_ref[...]
        out_refs[0][:, width:] = gmix
        return
    dp = lax.axis_index("dp")
    part = out_refs[0].shape[0]
    half = part // 2

    def put(ref, at, step, k, lo, rows):
        source = pl.multiple_of((dp ^ step) * part + lo, half)
        ref[at : at + rows, :width] = gw_ref[pl.ds(source, rows), :]
        if k is not None:
            ref[at : at + rows, width:] = gmix[k * part + lo : k * part + lo + rows]

    for ref, step in zip(out_refs, (0, 1, 2, 4)):
        put(ref, 0, step, None, 0, part)
    put(out_refs[4], 0, 5, 1, 0, part)
    put(out_refs[4], part, 3, 3, 0, half)
    put(out_refs[5], 0, 6, 2, 0, part)
    put(out_refs[5], part, 3, 3, half, half)
    put(out_refs[6], 0, 7, 0, 0, half)
    put(out_refs[7], 0, 7, 0, half, half)


def token_backward(keep_ref, core_ref, chip_ref, tok_ref, rows_ref, out_ref, grad_ref, resid):
    seq = lax.axis_index("seq")
    images, shard, features = tok_ref.shape
    total = keep_ref[0, :images].astype(F32) + core_ref[0, :images].astype(F32)
    total = (total + chip_ref[:images].astype(F32)).reshape(images * shard, features)
    for r, got in enumerate(
        (keep_ref.at[0, images:], core_ref.at[0, images:], chip_ref.at[images : images + 2],
         chip_ref.at[images + 2 :])
    ):
        out_ref[pl.ds(seq ^ r, 1)] = got[0:1]
        resid[pl.ds(seq ^ r, 1)] = got[1:2]
    normed, root = unit(tok_ref[...].astype(F32).reshape(images * shard, features))
    back = unit_back(total * rows_ref[0:1], normed, root).reshape(images, shard, features)
    grad_ref[...] = (resid[...].astype(F32) + back).astype(BF16)


def plus(a, b):
    return (a.astype(F32) + b.astype(F32)).astype(BF16)


def reduce_last(y_ref, z_ref, first_ref, second_ref, to_y, to_z):
    half = first_ref.shape[0]
    to_y[...] = y_ref[...]
    to_z[...] = z_ref[...]
    to_y[half : 2 * half, :] = plus(y_ref[half : 2 * half, :], second_ref[...])
    to_z[:half, :] = plus(z_ref[:half, :], first_ref[...])


def reduce_blocks(
    own_ref, beside_ref, across_ref, far_ref, y_ref, z_ref, mine_ref, other_ref,
    own, beside, across, far,
):
    part = far_ref.shape[0]
    half = part // 2
    gmix = both_chips(mine_ref, other_ref)
    width = far_ref.shape[1] - gmix.shape[1]

    def block(ref, k):
        return jnp.concatenate(
            [ref[:, :width].astype(F32), gmix[k * part : (k + 1) * part]], axis=1
        )

    beside_sum, across_sum, far_sum, own_sum = (
        block(ref, k) for k, ref in enumerate((beside_ref, across_ref, far_ref, own_ref))
    )
    own[...] = own_sum.astype(BF16)
    far_sum = far_sum + y_ref[:part, :].astype(F32) + z_ref[:part, :].astype(F32)
    far[...] = far_sum.astype(BF16)
    across[:half, :] = (across_sum[:half] + y_ref[part:, :].astype(F32)).astype(BF16)
    across[half:, :] = across_sum[half:].astype(BF16)
    beside[:half, :] = beside_sum[:half].astype(BF16)
    beside[half:, :] = (beside_sum[half:] + z_ref[part:, :].astype(F32)).astype(BF16)


def add_second(keep_ref, got_ref, out_ref):
    images = keep_ref.shape[1] - 2
    out_ref[:images] = (
        keep_ref[1, :images].astype(F32) + got_ref[1, :images].astype(F32)
    ).astype(BF16)
    out_ref[images : images + 2] = keep_ref[1, images:]
    out_ref[images + 2 :] = got_ref[1, images:]


def sum_parts(*refs):
    total = refs[0][...].astype(F32)
    for ref in refs[1:-1]:
        total = total + ref[...].astype(F32)
    refs[-1][...] = total.astype(BF16)


def spread_parts(groups, here, misc_w, experts):
    def kernel(*refs):
        in_refs = refs[:groups]
        qkv_ref, mix_ref, router_ref = refs[groups : groups + 3]
        row_refs = refs[groups + 3 :]
        features = mix_ref.shape[1]
        seq = lax.axis_index("seq")
        for s in range(groups):

            @pl.when(seq == s)
            def _():
                for r in range(groups):
                    g = s ^ r
                    for j in range(3):
                        lo = j * features + g * here
                        part = in_refs[r][:, j * here : (j + 1) * here]
                        qkv_ref[:, lo : lo + here] = part.astype(F32)
                    part = in_refs[r][:, 3 * here + misc_w :]
                    mix_ref[:, g * here : (g + 1) * here] = part.astype(F32)

        misc = in_refs[0][:, 3 * here : 3 * here + misc_w].astype(F32)
        for r in range(1, groups):
            misc = misc + in_refs[r][:, 3 * here : 3 * here + misc_w].astype(F32)
        misc = misc.T
        router_ref[...] = misc[:experts]
        for j in range(5):
            row_refs[j][...] = misc[experts + j : experts + j + 1]

    return kernel


def body(
    tokens,
    pad_mask,
    counts,
    attn_gain,
    attn_shift,
    qkv_weight,
    mix_weight,
    mix_bias,
    moe_gain,
    moe_shift,
    router,
    expert_in,
    hidden_bias,
    expert_out,
    output_bias,
    cotangent,
):
    images, shard, features = tokens.shape
    groups = lax.axis_size("seq")
    lanes = lax.axis_size("dp")
    devices = groups * lanes
    part = mix_weight.shape[0]
    experts = router.shape[1]
    hidden = expert_in.shape[2]
    misc_w = -(-(experts + 8) // 64) * 64
    here = HEADS // groups * HEAD_DIM
    wide = -(-here // 128) * 128
    half = features // 2
    full = groups * shard
    direct = lanes == 8 and part % 32 == 0
    piece_w = 3 * here + misc_w + here

    def swap(a, axis, step):
        return lax.ppermute(a, axis, [(i, i ^ step) for i in range(lax.axis_size(axis))])

    def exchange(parts):
        moved = {r: swap(parts[r], "seq", r) for r in range(groups - 1, 0, -1)}
        return [parts[0]] + [moved[r] for r in range(1, groups)]

    packed_w = 3 * here + misc_w + half
    (piece,) = kernel_call(
        pack_inputs(groups, here, half, misc_w, experts),
        [qkv_weight, router.T]
        + [v.reshape(1, part) for v in (attn_gain, attn_shift, mix_bias, moe_gain, moe_shift)]
        + [mix_weight],
        [((part, packed_w), BF16)],
        [pltpu.VMEM((misc_w, -(-part // 128) * 128), F32)],
        limit=ALL_VMEM,
        hbm_in=tuple(range(8)),
    )
    cots = exchange(
        kernel_call(by_image_owner, [cotangent], [((shard, features), BF16)] * groups, limit=4)
    )
    over = swap(tokens, "seq", 2)
    near = swap(tokens, "seq", 1)
    if direct:
        far, across, beside = (swap(piece, "dp", step) for step in (4, 2, 1))
        far, across, beside, over, cots[2] = lax.optimization_barrier(
            (far, across, beside, over, cots[2])
        )
        longer = ((part + part // 2, packed_w), BF16)
        to_y, to_z = kernel_call(forward_blocks, [beside, across, far], [longer] * 2, limit=4)
        by_y, by_z = swap(to_y, "dp", 1), swap(to_z, "dp", 2)
        by_y, by_z, near, cots[1], cots[3] = lax.optimization_barrier(
            (by_y, by_z, near, cots[1], cots[3])
        )
        a, b = kernel_call(forward_last, [by_y, by_z], [((part // 2, packed_w), BF16)] * 2, limit=4)
        piece_parts = [piece, beside, across, far, by_y, by_z, swap(a, "dp", 1), swap(b, "dp", 2)]
    else:
        piece_parts = [lax.all_gather(piece, "dp", axis=0, tiled=True)]
    normed, units, mine = kernel_call(
        normalize_tokens(groups),
        [tokens, near, over, swap(over, "seq", 1)],
        [
            ((images, ROWS, features), F32),
            ((images, ROWS, features), BF16),
            ((ROWS, features), BF16),
        ],
        [pltpu.VMEM((images, full, features), BF16)],
        limit=8,
        flops=1e8,
    )
    outs = kernel_call(
        attend_forward(groups, len(piece_parts), here, wide, misc_w, experts),
        [normed, pad_mask, counts] + piece_parts,
        [((FOLD, 2 * here), BF16)] * groups
        + [
            ((features, half), BF16),
            ((images, ROWS, HEADS // groups * full), BF16),
            ((images, ROWS, features), BF16),
            ((images, full, 3 * wide), BF16),
            ((features, 3 * wide), BF16),
            ((8, features), F32),
            ((features, experts), BF16),
        ],
        [
            pltpu.VMEM((features, packed_w), BF16),
            pltpu.VMEM((images, ROWS, here), BF16),
        ],
        smem=(2,),
        limit=16,
        flops=1e8,
    )
    sent = exchange(outs[:groups])
    mix_half, probs, xa, qkv, wpad, rows, router_full = outs[groups:]
    slots, resid, mixed, logits, mix_full, grad, heads = kernel_call(
        route_forward(groups, here, half),
        sent
        + cots
        + [mine, rows, router_full, pad_mask, counts, mix_half, swap(mix_half, "seq", 1)],
        [
            ((experts, 2, features), BF16),
            ((ROWS, features), F32),
            ((ROWS, features), BF16),
            ((ROWS, experts), F32),
            ((features, features), BF16),
            ((ROWS, features), BF16),
            ((groups, ROWS, here), BF16),
        ],
        [pltpu.VMEM((full, features), BF16)],
        smem=(2 * groups + 4,),
        limit=10,
        flops=5e9,
    )
    slots = lax.all_to_all(slots, ("dp", "seq"), split_axis=0, concat_axis=0, tiled=True)
    block = min(512, hidden)
    back, hid, grad_pre, grad_hidden_bias, grad_output_bias = kernel_call(
        expert_values,
        [slots, expert_in, hidden_bias, expert_out, output_bias],
        [
            ((devices, 2, features), BF16),
            ((devices, hidden), BF16),
            ((devices, hidden), BF16),
            ((1, hidden), F32),
            ((1, features), F32),
        ],
        limit=8,
        flops=5e9,
    )
    back = lax.all_to_all(back, ("dp", "seq"), split_axis=0, concat_axis=0, tiled=True)

    def expert_gradients(first, count, ins):
        lane_spec = pl.BlockSpec((devices, block), lambda i: (0, i + first))
        return pl.pallas_call(
            expert_weights,
            grid=(count,),
            in_specs=[pl.BlockSpec((devices, 2, features), lambda i: (0, 0, 0))]
            + [lane_spec] * 2
            + [pl.BlockSpec(memory_space=pl.ANY)] * (len(ins) - 3),
            out_specs=[
                pl.BlockSpec((1, features, block), lambda i: (0, 0, i + first)),
                pl.BlockSpec((1, block, features), lambda i: (0, i + first, 0)),
            ],
            out_shape=[
                jax.ShapeDtypeStruct((1, features, hidden), F32),
                jax.ShapeDtypeStruct((1, hidden, features), F32),
            ],
            input_output_aliases={i: i - 3 for i in range(3, len(ins))},
            compiler_params=pltpu.CompilerParams(vmem_limit_bytes=12 * 2**20),
            cost_estimate=pl.CostEstimate(
                flops=1 if first else 10**11, bytes_accessed=0, transcendentals=0
            ),
        )(*ins)

    steps = hidden // block
    early = steps // 3
    expert_grads = expert_gradients(0, early, [slots, hid, grad_pre])
    outs = kernel_call(
        route_backward(groups, here, misc_w, experts),
        [back, resid, mixed, logits, grad, mix_full, router_full, rows, pad_mask, counts, heads],
        [((FOLD, 2 * here), BF16)] * groups
        + [((2, full, features), BF16)]
        + [((features, groups // 2 * here), BF16)] * 2
        + [((misc_w, features), F32)],
        [pltpu.VMEM((features, features), BF16), pltpu.VMEM((misc_w, features), F32)],
        smem=(9,),
        limit=16,
        flops=5e9,
    )
    gheads = exchange(outs[:groups])
    token_rows, keep, send, misc = outs[groups:]
    mix_parts = ((7, 5, 6, 3), (1, 2, 4, 0)) if direct else ((0,),)
    size = part if direct else features
    count = size * len(mix_parts[0])
    outs_mix = kernel_call(
        add_shares(mix_parts, size),
        [keep, swap(send, "seq", 1)],
        [((count, here), BF16)] * len(mix_parts)
        + [((count // 2, 2 * here), BF16)] * len(mix_parts),
        [pltpu.VMEM((features, groups // 2 * here), BF16)],
        limit=8,
    )
    *outs_mix, own = lax.optimization_barrier(outs_mix + [gheads[0]])
    gmix, gmix_send = outs_mix[: len(mix_parts)], outs_mix[len(mix_parts) :]
    gmix_other = [swap(gmix_send[0], "seq", 2)]
    gqkv_spec = ((images * ROWS, 3 * wide), BF16)
    image_scratch = [
        pltpu.VMEM((ROWS, wide), BF16),
        pltpu.VMEM((ROWS, HEADS // groups * full), BF16),
    ]
    (gqkv,) = kernel_call(
        attend_backward_near(HEADS // groups),
        [own, gheads[1], qkv, probs],
        [gqkv_spec],
        image_scratch,
        limit=8,
        flops=1e10,
    )
    gqkv, gx, gx_send, gw = kernel_call(
        attend_backward_far(groups, here, wide, misc_w, experts),
        gheads[2:] + [qkv, probs, xa, units, wpad, misc, token_rows, gqkv],
        [
            gqkv_spec,
            ((2, images + 2, shard, features), BF16),
            ((2, images + 2, shard, features), BF16),
            ((features, 3 * here + misc_w), BF16),
        ],
        image_scratch
        + [
            pltpu.VMEM((images, full, features), BF16),
            pltpu.VMEM((misc_w, features), F32),
        ],
        limit=20,
        aliases={groups + 5: 0},
        flops=1e10,
    )
    gx_core = swap(gx_send, "seq", 1)
    whole = ((part, piece_w), BF16)
    longer = ((part + part // 2, piece_w), BF16)
    shorter = ((part // 2, piece_w), BF16)
    out_parts = [whole] * 4 + [longer] * 2 + [shorter] * 2
    if not direct:
        out_parts = [((features, piece_w), BF16)]
    outs = kernel_call(
        cut_gradients,
        [gw, gmix[0], gmix_other[0]],
        out_parts,
        limit=8,
        flops=2e10,
    )
    gx_core, _ = lax.optimization_barrier((gx_core, outs[0]))
    if direct:
        own, beside, across, far, to_y, to_z, first, second = outs
        first, second = swap(first, "dp", 1), swap(second, "dp", 2)
        late, _ = lax.optimization_barrier((gmix_send[1], gmix_other[0]))
        first, second, late, *expert_grads = lax.optimization_barrier(
            [first, second, swap(late, "seq", 2)] + list(expert_grads)
        )
        expert_grads = expert_gradients(early, steps - early, [slots, hid, grad_pre, *expert_grads])
        to_y, to_z = kernel_call(
            reduce_last, [to_y, to_z, first, second], [longer] * 2, limit=4
        )
        by_y, by_z = swap(to_y, "dp", 1), swap(to_z, "dp", 2)
        by_y, by_z, *expert_grads = lax.optimization_barrier([by_y, by_z] + list(expert_grads))
        own, beside, across, far = kernel_call(
            reduce_blocks,
            [own, beside, across, far, by_y, by_z, gmix[1], late],
            [whole] * 4,
            limit=8,
        )
        sums = [swap(far, "dp", 4), swap(across, "dp", 2), swap(beside, "dp", 1), own]
    else:
        expert_grads = expert_gradients(early, steps - early, [slots, hid, grad_pre, *expert_grads])
        arrived = lax.all_to_all(outs[0], "dp", split_axis=0, concat_axis=0, tiled=True)
        sums = [arrived[r * part : (r + 1) * part] for r in range(lanes)]
    (gx_sum,) = kernel_call(
        add_second, [gx, gx_core], [((images + 4, shard, features), BF16)], limit=4
    )
    gx_chip = swap(gx_sum, "seq", 2)
    (share,) = kernel_call(sum_parts, sums, [whole], limit=4)
    share, gx_chip = lax.optimization_barrier((share, gx_chip))
    block_out, input_grad = kernel_call(
        token_backward,
        [gx, gx_core, gx_chip, tokens, rows],
        [((images, shard, features), BF16), ((images, shard, features), BF16)],
        [pltpu.VMEM((images, shard, features), BF16)],
        limit=8,
        flops=2e9,
    )
    share_over = swap(share, "seq", 2)
    shares = [share, swap(share, "seq", 1), share_over, swap(share_over, "seq", 1)]
    grad_qkv, grad_mix, grad_router, *vector_rows = kernel_call(
        spread_parts(groups, here, misc_w, experts),
        shares,
        [((part, 3 * features), F32), ((part, features), F32), ((experts, part), F32)]
        + [((1, part), F32)] * 5,
        limit=8,
    )
    vector_rows = [v.reshape(part) for v in vector_rows]
    return (
        block_out,
        input_grad,
        vector_rows[0],
        vector_rows[1],
        grad_qkv,
        grad_mix,
        vector_rows[2],
        vector_rows[3],
        vector_rows[4],
        grad_router.T,
        expert_grads[0],
        grad_hidden_bias,
        expert_grads[1],
        grad_output_bias,
    )


def solution(mesh):
    return jax.shard_map(
        body,
        mesh=mesh,
        in_specs=(
            P("dp", "seq", None),
            P("dp", None),
            P("dp"),
            P("dp"),
            P("dp"),
            P("dp", None),
            P("dp", None),
            P("dp"),
            P("dp"),
            P("dp"),
            P("dp", None),
            P(("dp", "seq"), None, None),
            P(("dp", "seq"), None),
            P(("dp", "seq"), None, None),
            P(("dp", "seq"), None),
            P("dp", "seq", None),
        ),
        out_specs=(
            P("dp", "seq", None),
            P("dp", "seq", None),
            P("dp"),
            P("dp"),
            P("dp", None),
            P("dp", None),
            P("dp"),
            P("dp"),
            P("dp"),
            P("dp", None),
            P(("dp", "seq"), None, None),
            P(("dp", "seq"), None),
            P(("dp", "seq"), None, None),
            P(("dp", "seq"), None),
        ),
        check_vma=False,
    )
```

```python
import math

import jax
import jax.numpy as jnp
from jax import lax
from jax.experimental import pallas as pl
from jax.experimental.pallas import tpu as pltpu
from jax.sharding import PartitionSpec as P

HEADS = 12
HEAD_DIM = 64
EPS = 1e-06
NEG = -1000000000.0
BF16 = jnp.bfloat16
F32 = jnp.float32
ALL_VMEM = 62.6
FOLD = 112
ROWS = 208
NT = (((1,), (1,)), ((), ()))
TN = (((0,), (0,)), ((), ()))


def mm(a, b):
    return jnp.dot(a, b, preferred_element_type=F32)


def mm_nt(a, b):
    return lax.dot_general(a, b, NT, preferred_element_type=F32)


def mm_tn(a, b):
    return lax.dot_general(a, b, TN, preferred_element_type=F32)


def unit(values):
    center = values - jnp.mean(values, axis=-1, keepdims=True)
    spread = jnp.mean(center * center, axis=-1, keepdims=True)
    root = lax.rsqrt(spread + EPS)
    return center * root, root


def unit_back(scaled, rows, root):
    inner = jnp.mean(scaled * rows, axis=-1, keepdims=True)
    return root * (scaled - jnp.mean(scaled, axis=-1, keepdims=True) - rows * inner)


def lane_mask(index, width):
    lane = lax.broadcasted_iota(jnp.int32, (1, width), 1)
    return (lane >= index * HEAD_DIM) & (lane < (index + 1) * HEAD_DIM)


def image_length(mask_ref, counts_ref, image):
    which = lax.broadcasted_iota(jnp.int32, mask_ref.shape, 0)
    real = jnp.where(which == image, mask_ref[...], 0)
    total = jnp.sum(jnp.sum(real, axis=1, keepdims=True), axis=0, keepdims=True)
    return jnp.where(image < counts_ref[0], total, 0)


def kernel_call(
    kernel, ins, outs, scratch=(), limit=48, smem=(), hbm_in=(), hbm_out=(), aliases=None, flops=1
):
    kw = {
        "input_output_aliases": aliases or {},
        "cost_estimate": pl.CostEstimate(flops=int(flops), bytes_accessed=0, transcendentals=0),
    }
    n_in, n_out, n_own = len(ins), len(outs), len(scratch)
    n_staged = len(hbm_in) + len(hbm_out)

    def wrapped(*refs):
        in_refs = list(refs[:n_in])
        out_refs = list(refs[n_in : n_in + n_out])
        own = refs[n_in + n_out : n_in + n_out + n_own]
        stages = refs[n_in + n_out + n_own :]
        reads, writes = [], {}
        for j, i in enumerate(hbm_in):
            reads.append(pltpu.make_async_copy(in_refs[i], stages[j], stages[-1].at[j]))
            in_refs[i] = stages[j]
        for j, i in enumerate(hbm_out, len(hbm_in)):
            writes[i] = pltpu.make_async_copy(stages[j], out_refs[i], stages[-1].at[j])
            out_refs[i] = stages[j]
        for copy in reads:
            copy.start()
        for copy in reads:
            copy.wait()
        kernel(*in_refs, *out_refs, *own)
        for copy in writes.values():
            copy.start()
        for copy in writes.values():
            copy.wait()

    def spec(i, staged):
        if i in staged:
            return pl.BlockSpec(memory_space=pltpu.HBM)
        return pl.BlockSpec(memory_space=pltpu.VMEM)

    in_specs = [
        pl.BlockSpec(memory_space=pltpu.SMEM) if i in smem else spec(i, hbm_in)
        for i in range(n_in)
    ]
    scratch = list(scratch)
    scratch += [pltpu.VMEM(ins[i].shape, ins[i].dtype) for i in hbm_in]
    scratch += [pltpu.VMEM(*outs[i]) for i in hbm_out]
    if n_staged:
        scratch.append(pltpu.SemaphoreType.DMA((n_staged,)))
    call = pl.pallas_call(
        wrapped,
        in_specs=in_specs,
        out_specs=[spec(i, hbm_out) for i in range(n_out)],
        out_shape=[jax.ShapeDtypeStruct(shape, kind) for shape, kind in outs],
        scratch_shapes=scratch,
        compiler_params=pltpu.CompilerParams(vmem_limit_bytes=int(limit * 2**20)),
        **kw,
    )
    return list(call(*ins))


def place(full, refs, dp):
    if len(refs) == 1:
        full[...] = refs[0][...]
        return
    part = refs[0].shape[0]
    half = part // 2

    def put(ref, rows, step, lo):
        at = pl.multiple_of((dp ^ step) * part + lo, half)
        full[pl.ds(at, rows.stop - rows.start), :] = ref[rows, :]

    whole, rest = slice(0, part), slice(part, part + half)
    for ref, step in zip(refs, (0, 1, 2, 4, 5, 6)):
        put(ref, whole, step, 0)
    put(refs[4], rest, 3, 0)
    put(refs[5], rest, 3, half)
    put(refs[6], slice(0, half), 7, 0)
    put(refs[7], slice(0, half), 7, half)


def forward_blocks(beside, across, far, y_ref, z_ref):
    part = far.shape[0]
    half = part // 2
    y_ref[:part, :] = far[...]
    y_ref[part:, :] = across[:half, :]
    z_ref[:part, :] = far[...]
    z_ref[part:, :] = beside[half:, :]


def forward_last(y_ref, z_ref, first_ref, second_ref):
    half = first_ref.shape[0]
    first_ref[...] = z_ref[:half, :]
    second_ref[...] = y_ref[half : 2 * half, :]


def head_masks(width, heads_here):
    return [lane_mask(h, width) for h in range(heads_here)]


def pack_inputs(groups, here, half, misc_w, experts):
    def kernel(*refs):
        qkv_ref, router_ref = refs[:2]
        vectors = refs[2:7]
        mix_ref, piece_ref, turn = refs[7:]
        seq = lax.axis_index("seq")
        features = qkv_ref.shape[1] // 3
        part = qkv_ref.shape[0]
        for g in range(groups):

            @pl.when(seq == g)
            def _():
                for j in range(3):
                    lo = j * features + g * here
                    piece_ref[:, j * here : (j + 1) * here] = qkv_ref[:, lo : lo + here]

        turn[...] = jnp.zeros_like(turn)
        turn[:experts, :part] = router_ref[...].astype(F32)
        for j in range(5):
            turn[experts + j : experts + j + 1, :part] = vectors[j][...].astype(F32)
        lo = 3 * here + misc_w
        piece_ref[:, 3 * here : lo] = turn[...].T[:part].astype(BF16)
        piece_ref[:, lo:] = mix_ref[:, pl.ds(pl.multiple_of((seq & 1) * half, 128), half)]

    return kernel


def by_image_owner(cot_ref, *cot_refs):
    seq = lax.axis_index("seq")
    for r in range(len(cot_refs)):
        cot_refs[r][...] = cot_ref[pl.ds(seq ^ r, 1)][0]


def normalize_tokens(groups):
    def kernel(*refs):
        tok_refs = refs[:groups]
        normed_ref, unit_ref, mine_ref, tok = refs[groups:]
        seq = lax.axis_index("seq")
        images, shard, _ = tok_refs[0].shape
        for r in range(groups):
            rows = pl.ds(pl.multiple_of((seq ^ r) * shard, shard), shard)
            tok[:, rows, :] = tok_refs[r][...]
        mine_ref[...] = tok[pl.ds(seq, 1), :ROWS, :][0]
        for i in range(images):
            normed, _ = unit(tok[i, :ROWS, :].astype(F32))
            normed_ref[i] = normed
            unit_ref[i] = normed.astype(BF16)

    return kernel


def attend_forward(groups, pieces, here, wide, misc_w, experts):
    heads_here = HEADS // groups

    def kernel(*refs):
        normed_ref, mask_ref, counts_ref = refs[:3]
        w_refs = refs[3 : 3 + pieces]
        sent_refs = refs[3 + pieces : 3 + pieces + groups]
        rest = refs[3 + pieces + groups :]
        (half_ref, probs_ref, xa_ref, qkv_ref, wpad_ref, rows_ref, router_ref, dense, heads) = rest
        seq = lax.axis_index("seq")
        images, _, features = normed_ref.shape
        place(dense, w_refs, lax.axis_index("dp"))
        wpad_ref[...] = jnp.zeros_like(wpad_ref)
        for j in range(3):
            wpad_ref[:, j * wide : j * wide + here] = dense[:, j * here : (j + 1) * here]
        half_ref[...] = dense[:, 3 * here + misc_w :]
        misc = dense[:, 3 * here : 3 * here + misc_w]
        router_ref[...] = misc[:, :experts]
        rows_ref[...] = misc.astype(F32).T[experts : experts + 8]
        xa_ref[...] = (normed_ref[...] * rows_ref[0:1][None] + rows_ref[1:2][None]).astype(BF16)
        flat = xa_ref[...].reshape(images * ROWS, features)
        qkv_ref[:, :ROWS, :] = (
            mm(flat, wpad_ref[...]).astype(BF16).reshape(images, ROWS, 3 * wide)
        )
        keys = qkv_ref.shape[1]
        qkv_ref[:, ROWS:, :] = jnp.zeros((images, keys - ROWS, 3 * wide), BF16)
        place_of_key = lax.broadcasted_iota(jnp.int32, (1, keys), 1)
        for i in range(images):
            valid = place_of_key < image_length(mask_ref, counts_ref, i)
            q, k, v = head_stacks(qkv_ref, i, wide, heads_here)
            scores = mm_nt(q, k) * HEAD_DIM ** (-0.5)
            for h in range(heads_here):
                lanes = slice(h * keys, (h + 1) * keys)
                masked = jnp.where(valid, scores[:, lanes], NEG)
                top = jnp.exp(masked - jnp.max(masked, axis=-1, keepdims=True))
                total = jnp.sum(top, axis=-1, keepdims=True)
                probs_ref[i, :, lanes] = (top / total).astype(BF16)
            heads[i] = mm(probs_ref[i], v)[:, :here].astype(BF16)
        for r in range(groups):
            fold(sent_refs[r], heads[pl.ds(seq ^ r, 1)][0])

    return kernel


def head_stacks(qkv_ref, image, wide, heads_here):
    masks = head_masks(wide, heads_here)
    stacks = []
    for j in (1, 2):
        rows = qkv_ref[image, :, j * wide : (j + 1) * wide]
        stacks.append(jnp.concatenate([jnp.where(m, rows, jnp.zeros_like(rows)) for m in masks]))
    return qkv_ref[image, :ROWS, :wide], stacks[0], stacks[1]


def fold(ref, rows):
    top, width = ref.shape[0], rows.shape[1]
    ref[:, :width] = rows[:top]
    ref[: rows.shape[0] - top, width:] = rows[top:]


def unfold(ref, part, count):
    width = ref.shape[1] // 2
    if part == 0:
        return ref[:, :width]
    return ref[: count - ref.shape[0], width:]


def head_rows(seq, r, here):
    return pl.ds(pl.multiple_of((seq ^ r) * here, here), here)


def route_forward(groups, here, half):
    def kernel(*refs):
        sent_refs = [refs[0], *refs[groups - 1 : 0 : -1]]
        cot_refs = refs[groups : 2 * groups]
        mine_ref, rows_ref, router_ref, mask_ref, counts_ref = refs[2 * groups : 2 * groups + 5]
        half_refs = refs[2 * groups + 5 : -8]
        slots_ref, resid_ref, mixed_ref, logits_ref, mix_ref, grad_ref, heads_ref, cot = refs[-8:]
        seq = lax.axis_index("seq")
        for j in range(2):
            lanes = pl.ds(pl.multiple_of(((seq & 1) ^ j) * half, 128), half)
            mix_ref[:, lanes] = half_refs[j][...]
        for r in range(groups):
            heads_ref[r, :FOLD] = unfold(sent_refs[r], 0, ROWS)
            heads_ref[r, FOLD:] = unfold(sent_refs[r], 1, ROWS)
            shard = cot_refs[r].shape[0]
            cot[pl.ds(pl.multiple_of((seq ^ r) * shard, shard), shard), :] = cot_refs[r][...]
        resid = mine_ref[...].astype(F32) + rows_ref[2:3]
        for r in range(groups):
            resid = resid + mm(heads_ref[r], mix_ref[head_rows(seq, r, here), :])
        resid_ref[...] = resid
        normed, _ = unit(resid)
        mixed = (normed * rows_ref[3:4] + rows_ref[4:5]).astype(BF16)
        mixed_ref[...] = mixed
        logits = mm(mixed, router_ref[...])
        logits_ref[...] = logits
        length = image_length(mask_ref, counts_ref, seq)
        valid = lax.broadcasted_iota(jnp.int32, (ROWS, 1), 0) < length
        dispatch = token_softmax(logits, valid)
        combine = slot_softmax(logits)
        grad = cot[:ROWS, :]
        grad = jnp.where(valid, grad, jnp.zeros_like(grad))
        grad_ref[...] = grad
        slots_ref[:, 0, :] = mm_tn(dispatch.astype(BF16), mixed).astype(BF16)
        slots_ref[:, 1, :] = mm_tn(combine.astype(BF16), grad).astype(BF16)

    return kernel


def token_softmax(logits, valid):
    masked = jnp.where(valid, logits, NEG)
    top = jnp.exp(masked - jnp.max(masked, axis=0, keepdims=True))
    return top / jnp.sum(top, axis=0, keepdims=True)


def slot_softmax(logits):
    top = jnp.exp(logits - jnp.max(logits, axis=-1, keepdims=True))
    return top / jnp.sum(top, axis=-1, keepdims=True)


def expert_values(
    x_ref, win_ref, bias_ref, wout_ref, obias_ref, back_ref, hid_ref, pre_ref, hb_ref, ob_ref
):
    x = x_ref[:, 0, :]
    g = x_ref[:, 1, :]
    ob_ref[...] = jnp.sum(g.astype(F32), axis=0, keepdims=True)
    pre = mm(x, win_ref[0]) + bias_ref[...].astype(F32)
    phi = 0.5 * (1.0 + lax.erf(pre * 2.0 ** (-0.5)))
    hidden = (pre * phi).astype(BF16)
    hid_ref[...] = hidden
    back_ref[:, 0, :] = (mm(hidden, wout_ref[0]) + obias_ref[...].astype(F32)).astype(BF16)
    slope = phi + pre * jnp.exp(-0.5 * pre * pre) * (2.0 * math.pi) ** (-0.5)
    grad_pre = (mm_nt(g, wout_ref[0]) * slope).astype(BF16)
    pre_ref[...] = grad_pre
    hb_ref[...] = jnp.sum(grad_pre.astype(F32), axis=0, keepdims=True)
    back_ref[:, 1, :] = mm_nt(grad_pre, win_ref[0]).astype(BF16)


def expert_weights(x_ref, hid_ref, pre_ref, *refs):
    gin_ref, gout_ref = refs[-2:]
    gin_ref[0] = mm_tn(x_ref[:, 0, :], pre_ref[...])
    gout_ref[0] = mm_tn(hid_ref[...], x_ref[:, 1, :])


def route_backward(groups, here, misc_w, experts):
    def kernel(*refs):
        (back_ref, resid_ref, mixed_ref, logits_ref, grad_ref, mix_ref, router_ref, rows_ref) = (
            refs[:8]
        )
        mask_ref, counts_ref = refs[8:10]
        heads_ref = refs[10]
        rest = refs[11:]
        gheads_refs = rest[:groups]
        tok, keep_ref, send_ref, misc_ref, full, turn = rest[groups:]
        seq = lax.axis_index("seq")
        length = image_length(mask_ref, counts_ref, seq)
        valid = lax.broadcasted_iota(jnp.int32, (ROWS, 1), 0) < length
        logits = logits_ref[...]
        dispatch = token_softmax(logits, valid)
        combine = slot_softmax(logits)
        resid = resid_ref[...]
        mixed = mixed_ref[...]
        slot_out = back_ref[:, 0, :]
        grad_slot = back_ref[:, 1, :]
        grad = grad_ref[...]
        out = jnp.where(valid, resid + mm(combine.astype(BF16), slot_out), 0.0).astype(BF16)
        grad_combine = mm_nt(grad, slot_out)
        grad_dispatch = mm_nt(mixed, grad_slot)
        grad_logits = combine * (
            grad_combine - jnp.sum(combine * grad_combine, axis=-1, keepdims=True)
        ) + dispatch * (grad_dispatch - jnp.sum(dispatch * grad_dispatch, axis=0, keepdims=True))
        low = grad_logits.astype(BF16)
        grad_mixed = mm(dispatch.astype(BF16), grad_slot) + mm_nt(low, router_ref[...])
        normed, root = unit(resid)
        turn[...] = jnp.zeros_like(turn)
        turn[experts + 3 : experts + 4, :] = jnp.sum(grad_mixed * normed, axis=0, keepdims=True)
        turn[experts + 4 : experts + 5, :] = jnp.sum(grad_mixed, axis=0, keepdims=True)
        grad_resid = grad.astype(F32) + unit_back(grad_mixed * rows_ref[3:4], normed, root)
        turn[experts + 2 : experts + 3, :] = jnp.sum(grad_resid, axis=0, keepdims=True)
        turn[:experts, :] = mm_tn(low, mixed)
        misc_ref[...] = turn[...]
        gr = grad_resid.astype(BF16)
        tok[...] = jnp.zeros_like(tok)
        tok[0, :ROWS, :] = out
        tok[1, :ROWS, :] = gr
        for r in range(groups):
            fold(gheads_refs[r], mm_nt(gr, mix_ref[head_rows(seq, r, here), :]).astype(BF16))
            full[head_rows(seq, r, here), :] = mm_tn(heads_ref[r], gr).astype(BF16)
        for core in range(2):

            @pl.when((seq & 1) == core)
            def _():
                for j in range(groups // 2):
                    lanes = slice(j * here, (j + 1) * here)
                    lo = (2 * j + core) * here
                    keep_ref[:, lanes] = full[:, lo : lo + here]
                    lo = (2 * j + 1 - core) * here
                    send_ref[:, lanes] = full[:, lo : lo + here]

    return kernel


def add_shares(parts, size):
    def kernel(keep_ref, got_ref, *refs):
        mine_refs, send_refs = refs[: len(parts)], refs[len(parts) : -1]
        total = refs[-1]
        total[...] = (keep_ref[...].astype(F32) + got_ref[...].astype(F32)).astype(BF16)
        chip = lax.axis_index("seq") // 2
        dp = lax.axis_index("dp")
        width = mine_refs[0].shape[1]

        def block(step, lanes):
            if size == total.shape[0]:
                return total[:, lanes]
            return total[pl.ds(pl.multiple_of((dp ^ step) * size, size), size), lanes]

        for j in range(2):

            @pl.when(chip == j)
            def _():
                own, other = (slice(to * width, (to + 1) * width) for to in (j, 1 - j))
                for steps, mine, send in zip(parts, mine_refs, send_refs):
                    for k, step in enumerate(steps):
                        mine[k * size : (k + 1) * size, :] = block(step, own)
                    fold(send, jnp.concatenate([block(step, other) for step in steps]))

    return kernel


def both_chips(mine_ref, other_ref):
    count, half = mine_ref.shape[0], other_ref.shape[0]
    return jnp.concatenate(
        [
            mine_ref[:half, :].astype(F32) + unfold(other_ref, 0, count).astype(F32),
            mine_ref[half:, :].astype(F32) + unfold(other_ref, 1, count).astype(F32),
        ]
    )


def image_backward(gheads_ref, image, qkv_ref, probs_ref, gqkv, gh, gs, heads_here):
    keys = qkv_ref.shape[1]
    wide = gh.shape[1]
    here = gheads_ref.shape[1] // 2
    masks = head_masks(wide, heads_here)
    scaling = HEAD_DIM ** (-0.5)
    gh[:FOLD, :here] = unfold(gheads_ref, 0, ROWS)
    gh[FOLD:, :here] = unfold(gheads_ref, 1, ROWS)

    def by_head(stacked):
        picked = stacked[(heads_here - 1) * keys : (heads_here - 1) * keys + ROWS]
        for h in range(heads_here - 1):
            picked = jnp.where(masks[h], stacked[h * keys : h * keys + ROWS], picked)
        return picked

    q, k, v = head_stacks(qkv_ref, image, wide, heads_here)
    go = gh[...]
    gp = mm_nt(go, v)
    for h in range(heads_here):
        lanes = slice(h * keys, (h + 1) * keys)
        probs = probs_ref[image, :, lanes].astype(F32)
        inner = jnp.sum(probs * gp[:, lanes], axis=-1, keepdims=True)
        gs[:, lanes] = (probs * (gp[:, lanes] - inner)).astype(BF16)
    rows = pl.ds(pl.multiple_of(image * ROWS, ROWS), ROWS)
    gqkv[rows, :wide] = (mm(gs[...], k) * scaling).astype(BF16)
    gqkv[rows, wide : 2 * wide] = (by_head(mm_tn(gs[...], q)) * scaling).astype(BF16)
    gqkv[rows, 2 * wide :] = by_head(mm_tn(probs_ref[image], go)).astype(BF16)


def attend_backward_near(heads_here):
    def kernel(own_ref, near_ref, qkv_ref, probs_ref, gqkv, gh, gs):
        seq = lax.axis_index("seq")
        gh[...] = jnp.zeros_like(gh)
        for r, ref in enumerate((own_ref, near_ref)):
            image_backward(ref, seq ^ r, qkv_ref, probs_ref, gqkv, gh, gs, heads_here)

    return kernel


def attend_backward_far(groups, here, wide, misc_w, experts):
    heads_here = HEADS // groups

    def kernel(*refs):
        gheads_refs = refs[groups - 3 :: -1]
        qkv_ref, probs_ref, xa_ref, unit_ref, wpad_ref, misc_ref, token_ref = refs[
            groups - 2 : groups + 5
        ]
        gqkv, keep_ref, send_ref, gw_ref, gh, gs, gxs, turn = refs[groups + 6 :]
        images, _, features = unit_ref.shape
        seq = lax.axis_index("seq")
        gh[...] = jnp.zeros_like(gh)
        for j, ref in enumerate(gheads_refs):
            image_backward(ref, seq ^ (j + 2), qkv_ref, probs_ref, gqkv, gh, gs, heads_here)
        gx = mm_nt(gqkv[...], wpad_ref[...])
        shard = keep_ref.shape[2]
        gxs[:, :ROWS, :] = gx.astype(BF16).reshape(images, ROWS, features)
        gxs[:, ROWS:, :] = jnp.zeros((images, gxs.shape[1] - ROWS, features), BF16)
        for j in range(2):
            for to, ref in ((seq ^ (2 * j), keep_ref), (seq ^ (2 * j + 1), send_ref)):
                rows = pl.ds(pl.multiple_of(to * shard, shard), shard)
                ref[j, :images] = gxs[:, rows, :]
                ref[j, images:] = token_ref[:, rows, :]
        normed = unit_ref[...].reshape(images * ROWS, features).astype(F32)
        turn[...] = misc_ref[...]
        turn[experts : experts + 1, :] = jnp.sum(gx * normed, axis=0, keepdims=True)
        turn[experts + 1 : experts + 2, :] = jnp.sum(gx, axis=0, keepdims=True)
        gw_ref[:, 3 * here :] = turn[...].T.astype(BF16)
        gw = mm_tn(xa_ref[...].reshape(images * ROWS, features), gqkv[...]).astype(BF16)
        for j in range(3):
            gw_ref[:, j * here : (j + 1) * here] = gw[:, j * wide : j * wide + here]

    return kernel


def cut_gradients(gw_ref, mine_ref, other_ref, *out_refs):
    width = gw_ref.shape[1]
    gmix = both_chips(mine_ref, other_ref).astype(BF16)
    if len(out_refs) == 1:
        out_refs[0][:, :width] = gw_ref[...]
        out_refs[0][:, width:] = gmix
        return
    dp = lax.axis_index("dp")
    part = out_refs[0].shape[0]
    half = part // 2

    def put(ref, at, step, k, lo, rows):
        source = pl.multiple_of((dp ^ step) * part + lo, half)
        ref[at : at + rows, :width] = gw_ref[pl.ds(source, rows), :]
        if k is not None:
            ref[at : at + rows, width:] = gmix[k * part + lo : k * part + lo + rows]

    for ref, step in zip(out_refs, (0, 1, 2, 4)):
        put(ref, 0, step, None, 0, part)
    put(out_refs[4], 0, 5, 1, 0, part)
    put(out_refs[4], part, 3, 3, 0, half)
    put(out_refs[5], 0, 6, 2, 0, part)
    put(out_refs[5], part, 3, 3, half, half)
    put(out_refs[6], 0, 7, 0, 0, half)
    put(out_refs[7], 0, 7, 0, half, half)


def token_backward(keep_ref, core_ref, chip_ref, tok_ref, rows_ref, out_ref, grad_ref, resid):
    seq = lax.axis_index("seq")
    images, shard, features = tok_ref.shape
    total = keep_ref[0, :images].astype(F32) + core_ref[0, :images].astype(F32)
    total = (total + chip_ref[:images].astype(F32)).reshape(images * shard, features)
    for r, got in enumerate(
        (keep_ref.at[0, images:], core_ref.at[0, images:], chip_ref.at[images : images + 2],
         chip_ref.at[images + 2 :])
    ):
        out_ref[pl.ds(seq ^ r, 1)] = got[0:1]
        resid[pl.ds(seq ^ r, 1)] = got[1:2]
    normed, root = unit(tok_ref[...].astype(F32).reshape(images * shard, features))
    back = unit_back(total * rows_ref[0:1], normed, root).reshape(images, shard, features)
    grad_ref[...] = (resid[...].astype(F32) + back).astype(BF16)


def plus(a, b):
    return (a.astype(F32) + b.astype(F32)).astype(BF16)


def reduce_last(y_ref, z_ref, first_ref, second_ref, to_y, to_z):
    half = first_ref.shape[0]
    to_y[...] = y_ref[...]
    to_z[...] = z_ref[...]
    to_y[half : 2 * half, :] = plus(y_ref[half : 2 * half, :], second_ref[...])
    to_z[:half, :] = plus(z_ref[:half, :], first_ref[...])


def reduce_blocks(
    own_ref, beside_ref, across_ref, far_ref, y_ref, z_ref, mine_ref, other_ref,
    own, beside, across, far,
):
    part = far_ref.shape[0]
    half = part // 2
    gmix = both_chips(mine_ref, other_ref)
    width = far_ref.shape[1] - gmix.shape[1]

    def block(ref, k):
        return jnp.concatenate(
            [ref[:, :width].astype(F32), gmix[k * part : (k + 1) * part]], axis=1
        )

    beside_sum, across_sum, far_sum, own_sum = (
        block(ref, k) for k, ref in enumerate((beside_ref, across_ref, far_ref, own_ref))
    )
    own[...] = own_sum.astype(BF16)
    far_sum = far_sum + y_ref[:part, :].astype(F32) + z_ref[:part, :].astype(F32)
    far[...] = far_sum.astype(BF16)
    across[:half, :] = (across_sum[:half] + y_ref[part:, :].astype(F32)).astype(BF16)
    across[half:, :] = across_sum[half:].astype(BF16)
    beside[:half, :] = beside_sum[:half].astype(BF16)
    beside[half:, :] = (beside_sum[half:] + z_ref[part:, :].astype(F32)).astype(BF16)


def add_second(keep_ref, got_ref, out_ref):
    images = keep_ref.shape[1] - 2
    out_ref[:images] = (
        keep_ref[1, :images].astype(F32) + got_ref[1, :images].astype(F32)
    ).astype(BF16)
    out_ref[images : images + 2] = keep_ref[1, images:]
    out_ref[images + 2 :] = got_ref[1, images:]


def sum_parts(*refs):
    total = refs[0][...].astype(F32)
    for ref in refs[1:-1]:
        total = total + ref[...].astype(F32)
    refs[-1][...] = total.astype(BF16)


def spread_parts(groups, here, misc_w, experts):
    def kernel(*refs):
        in_refs = refs[:groups]
        qkv_ref, mix_ref, router_ref = refs[groups : groups + 3]
        row_refs = refs[groups + 3 :]
        features = mix_ref.shape[1]
        seq = lax.axis_index("seq")
        for s in range(groups):

            @pl.when(seq == s)
            def _():
                for r in range(groups):
                    g = s ^ r
                    for j in range(3):
                        lo = j * features + g * here
                        part = in_refs[r][:, j * here : (j + 1) * here]
                        qkv_ref[:, lo : lo + here] = part.astype(F32)
                    part = in_refs[r][:, 3 * here + misc_w :]
                    mix_ref[:, g * here : (g + 1) * here] = part.astype(F32)

        misc = in_refs[0][:, 3 * here : 3 * here + misc_w].astype(F32)
        for r in range(1, groups):
            misc = misc + in_refs[r][:, 3 * here : 3 * here + misc_w].astype(F32)
        misc = misc.T
        router_ref[...] = misc[:experts]
        for j in range(5):
            row_refs[j][...] = misc[experts + j : experts + j + 1]

    return kernel


def body(
    tokens,
    pad_mask,
    counts,
    attn_gain,
    attn_shift,
    qkv_weight,
    mix_weight,
    mix_bias,
    moe_gain,
    moe_shift,
    router,
    expert_in,
    hidden_bias,
    expert_out,
    output_bias,
    cotangent,
):
    images, shard, features = tokens.shape
    groups = lax.axis_size("seq")
    lanes = lax.axis_size("dp")
    devices = groups * lanes
    part = mix_weight.shape[0]
    experts = router.shape[1]
    hidden = expert_in.shape[2]
    misc_w = -(-(experts + 8) // 64) * 64
    here = HEADS // groups * HEAD_DIM
    wide = -(-here // 128) * 128
    half = features // 2
    full = groups * shard
    direct = lanes == 8 and part % 32 == 0
    piece_w = 3 * here + misc_w + here

    def swap(a, axis, step):
        return lax.ppermute(a, axis, [(i, i ^ step) for i in range(lax.axis_size(axis))])

    def exchange(parts):
        moved = {r: swap(parts[r], "seq", r) for r in range(groups - 1, 0, -1)}
        return [parts[0]] + [moved[r] for r in range(1, groups)]

    packed_w = 3 * here + misc_w + half
    (piece,) = kernel_call(
        pack_inputs(groups, here, half, misc_w, experts),
        [qkv_weight, router.T]
        + [v.reshape(1, part) for v in (attn_gain, attn_shift, mix_bias, moe_gain, moe_shift)]
        + [mix_weight],
        [((part, packed_w), BF16)],
        [pltpu.VMEM((misc_w, -(-part // 128) * 128), F32)],
        limit=ALL_VMEM,
        hbm_in=tuple(range(8)),
    )
    cots = exchange(
        kernel_call(by_image_owner, [cotangent], [((shard, features), BF16)] * groups, limit=4)
    )
    over = swap(tokens, "seq", 2)
    near = swap(tokens, "seq", 1)
    if direct:
        far, across, beside = (swap(piece, "dp", step) for step in (4, 2, 1))
        far, across, beside, over, cots[2] = lax.optimization_barrier(
            (far, across, beside, over, cots[2])
        )
        longer = ((part + part // 2, packed_w), BF16)
        to_y, to_z = kernel_call(forward_blocks, [beside, across, far], [longer] * 2, limit=4)
        by_y, by_z = swap(to_y, "dp", 1), swap(to_z, "dp", 2)
        by_y, by_z, near, cots[1], cots[3] = lax.optimization_barrier(
            (by_y, by_z, near, cots[1], cots[3])
        )
        a, b = kernel_call(forward_last, [by_y, by_z], [((part // 2, packed_w), BF16)] * 2, limit=4)
        piece_parts = [piece, beside, across, far, by_y, by_z, swap(a, "dp", 1), swap(b, "dp", 2)]
    else:
        piece_parts = [lax.all_gather(piece, "dp", axis=0, tiled=True)]
    normed, units, mine = kernel_call(
        normalize_tokens(groups),
        [tokens, near, over, swap(over, "seq", 1)],
        [
            ((images, ROWS, features), F32),
            ((images, ROWS, features), BF16),
            ((ROWS, features), BF16),
        ],
        [pltpu.VMEM((images, full, features), BF16)],
        limit=8,
        flops=1e8,
    )
    outs = kernel_call(
        attend_forward(groups, len(piece_parts), here, wide, misc_w, experts),
        [normed, pad_mask, counts] + piece_parts,
        [((FOLD, 2 * here), BF16)] * groups
        + [
            ((features, half), BF16),
            ((images, ROWS, HEADS // groups * full), BF16),
            ((images, ROWS, features), BF16),
            ((images, full, 3 * wide), BF16),
            ((features, 3 * wide), BF16),
            ((8, features), F32),
            ((features, experts), BF16),
        ],
        [
            pltpu.VMEM((features, packed_w), BF16),
            pltpu.VMEM((images, ROWS, here), BF16),
        ],
        smem=(2,),
        limit=16,
        flops=1e8,
    )
    sent = exchange(outs[:groups])
    mix_half, probs, xa, qkv, wpad, rows, router_full = outs[groups:]
    slots, resid, mixed, logits, mix_full, grad, heads = kernel_call(
        route_forward(groups, here, half),
        [sent[0], *sent[:0:-1]]
        + cots
        + [mine, rows, router_full, pad_mask, counts, mix_half, swap(mix_half, "seq", 1)],
        [
            ((experts, 2, features), BF16),
            ((ROWS, features), F32),
            ((ROWS, features), BF16),
            ((ROWS, experts), F32),
            ((features, features), BF16),
            ((ROWS, features), BF16),
            ((groups, ROWS, here), BF16),
        ],
        [pltpu.VMEM((full, features), BF16)],
        smem=(2 * groups + 4,),
        limit=10,
        flops=5e9,
    )
    slots = lax.all_to_all(slots, ("dp", "seq"), split_axis=0, concat_axis=0, tiled=True)
    block = min(512, hidden)
    back, hid, grad_pre, grad_hidden_bias, grad_output_bias = kernel_call(
        expert_values,
        [slots, expert_in, hidden_bias, expert_out, output_bias],
        [
            ((devices, 2, features), BF16),
            ((devices, hidden), BF16),
            ((devices, hidden), BF16),
            ((1, hidden), F32),
            ((1, features), F32),
        ],
        limit=8,
        flops=5e9,
    )
    back = lax.all_to_all(back, ("dp", "seq"), split_axis=0, concat_axis=0, tiled=True)

    def expert_gradients(first, count, ins):
        lane_spec = pl.BlockSpec((devices, block), lambda i: (0, i + first))
        return pl.pallas_call(
            expert_weights,
            grid=(count,),
            in_specs=[pl.BlockSpec((devices, 2, features), lambda i: (0, 0, 0))]
            + [lane_spec] * 2
            + [pl.BlockSpec(memory_space=pl.ANY)] * (len(ins) - 3),
            out_specs=[
                pl.BlockSpec((1, features, block), lambda i: (0, 0, i + first)),
                pl.BlockSpec((1, block, features), lambda i: (0, i + first, 0)),
            ],
            out_shape=[
                jax.ShapeDtypeStruct((1, features, hidden), F32),
                jax.ShapeDtypeStruct((1, hidden, features), F32),
            ],
            input_output_aliases={i: i - 3 for i in range(3, len(ins))},
            compiler_params=pltpu.CompilerParams(vmem_limit_bytes=12 * 2**20),
            cost_estimate=pl.CostEstimate(
                flops=1 if first else 10**11, bytes_accessed=0, transcendentals=0
            ),
        )(*ins)

    steps = hidden // block
    early = steps // 3
    expert_grads = expert_gradients(0, early, [slots, hid, grad_pre])
    outs = kernel_call(
        route_backward(groups, here, misc_w, experts),
        [back, resid, mixed, logits, grad, mix_full, router_full, rows, pad_mask, counts, heads],
        [((FOLD, 2 * here), BF16)] * groups
        + [((2, full, features), BF16)]
        + [((features, groups // 2 * here), BF16)] * 2
        + [((misc_w, features), F32)],
        [pltpu.VMEM((features, features), BF16), pltpu.VMEM((misc_w, features), F32)],
        smem=(9,),
        limit=16,
        flops=5e9,
    )
    gheads = exchange(outs[:groups])
    token_rows, keep, send, misc = outs[groups:]
    mix_parts = ((7, 5, 6, 3), (1, 2, 4, 0)) if direct else ((0,),)
    size = part if direct else features
    count = size * len(mix_parts[0])
    outs_mix = kernel_call(
        add_shares(mix_parts, size),
        [keep, swap(send, "seq", 1)],
        [((count, here), BF16)] * len(mix_parts)
        + [((count // 2, 2 * here), BF16)] * len(mix_parts),
        [pltpu.VMEM((features, groups // 2 * here), BF16)],
        limit=8,
    )
    *outs_mix, own = lax.optimization_barrier(outs_mix + [gheads[0]])
    gmix, gmix_send = outs_mix[: len(mix_parts)], outs_mix[len(mix_parts) :]
    gmix_other = [swap(gmix_send[0], "seq", 2)]
    gqkv_spec = ((images * ROWS, 3 * wide), BF16)
    image_scratch = [
        pltpu.VMEM((ROWS, wide), BF16),
        pltpu.VMEM((ROWS, HEADS // groups * full), BF16),
    ]
    (gqkv,) = kernel_call(
        attend_backward_near(HEADS // groups),
        [own, gheads[1], qkv, probs],
        [gqkv_spec],
        image_scratch,
        limit=8,
        flops=1e10,
    )
    gqkv, gx, gx_send, gw = kernel_call(
        attend_backward_far(groups, here, wide, misc_w, experts),
        gheads[:1:-1] + [qkv, probs, xa, units, wpad, misc, token_rows, gqkv],
        [
            gqkv_spec,
            ((2, images + 2, shard, features), BF16),
            ((2, images + 2, shard, features), BF16),
            ((features, 3 * here + misc_w), BF16),
        ],
        image_scratch
        + [
            pltpu.VMEM((images, full, features), BF16),
            pltpu.VMEM((misc_w, features), F32),
        ],
        limit=20,
        aliases={groups + 5: 0},
        flops=1e10,
    )
    gx_core = swap(gx_send, "seq", 1)
    whole = ((part, piece_w), BF16)
    longer = ((part + part // 2, piece_w), BF16)
    shorter = ((part // 2, piece_w), BF16)
    out_parts = [whole] * 4 + [longer] * 2 + [shorter] * 2
    if not direct:
        out_parts = [((features, piece_w), BF16)]
    outs = kernel_call(
        cut_gradients,
        [gw, gmix[0], gmix_other[0]],
        out_parts,
        limit=8,
        flops=2e10,
    )
    gx_core, _ = lax.optimization_barrier((gx_core, outs[0]))
    if direct:
        own, beside, across, far, to_y, to_z, first, second = outs
        first, second = swap(first, "dp", 1), swap(second, "dp", 2)
        late, _ = lax.optimization_barrier((gmix_send[1], gmix_other[0]))
        first, second, late, *expert_grads = lax.optimization_barrier(
            [first, second, swap(late, "seq", 2)] + list(expert_grads)
        )
        expert_grads = expert_gradients(early, steps - early, [slots, hid, grad_pre, *expert_grads])
        to_y, to_z = kernel_call(
            reduce_last, [to_y, to_z, first, second], [longer] * 2, limit=4
        )
        by_y, by_z = swap(to_y, "dp", 1), swap(to_z, "dp", 2)
        by_y, by_z, *expert_grads = lax.optimization_barrier([by_y, by_z] + list(expert_grads))
        own, beside, across, far = kernel_call(
            reduce_blocks,
            [own, beside, across, far, by_y, by_z, gmix[1], late],
            [whole] * 4,
            limit=8,
        )
        sums = [swap(far, "dp", 4), swap(across, "dp", 2), swap(beside, "dp", 1), own]
    else:
        expert_grads = expert_gradients(early, steps - early, [slots, hid, grad_pre, *expert_grads])
        arrived = lax.all_to_all(outs[0], "dp", split_axis=0, concat_axis=0, tiled=True)
        sums = [arrived[r * part : (r + 1) * part] for r in range(lanes)]
    (gx_sum,) = kernel_call(
        add_second, [gx, gx_core], [((images + 4, shard, features), BF16)], limit=4
    )
    gx_chip = swap(gx_sum, "seq", 2)
    (share,) = kernel_call(sum_parts, sums, [whole], limit=4)
    share, gx_chip = lax.optimization_barrier((share, gx_chip))
    block_out, input_grad = kernel_call(
        token_backward,
        [gx, gx_core, gx_chip, tokens, rows],
        [((images, shard, features), BF16), ((images, shard, features), BF16)],
        [pltpu.VMEM((images, shard, features), BF16)],
        limit=8,
        flops=2e9,
    )
    share_over = swap(share, "seq", 2)
    shares = [share, swap(share, "seq", 1), share_over, swap(share_over, "seq", 1)]
    grad_qkv, grad_mix, grad_router, *vector_rows = kernel_call(
        spread_parts(groups, here, misc_w, experts),
        shares,
        [((part, 3 * features), F32), ((part, features), F32), ((experts, part), F32)]
        + [((1, part), F32)] * 5,
        limit=8,
    )
    vector_rows = [v.reshape(part) for v in vector_rows]
    return (
        block_out,
        input_grad,
        vector_rows[0],
        vector_rows[1],
        grad_qkv,
        grad_mix,
        vector_rows[2],
        vector_rows[3],
        vector_rows[4],
        grad_router.T,
        expert_grads[0],
        grad_hidden_bias,
        expert_grads[1],
        grad_output_bias,
    )


def solution(mesh):
    return jax.shard_map(
        body,
        mesh=mesh,
        in_specs=(
            P("dp", "seq", None),
            P("dp", None),
            P("dp"),
            P("dp"),
            P("dp"),
            P("dp", None),
            P("dp", None),
            P("dp"),
            P("dp"),
            P("dp"),
            P("dp", None),
            P(("dp", "seq"), None, None),
            P(("dp", "seq"), None),
            P(("dp", "seq"), None, None),
            P(("dp", "seq"), None),
            P("dp", "seq", None),
        ),
        out_specs=(
            P("dp", "seq", None),
            P("dp", "seq", None),
            P("dp"),
            P("dp"),
            P("dp", None),
            P("dp", None),
            P("dp"),
            P("dp"),
            P("dp"),
            P("dp", None),
            P(("dp", "seq"), None, None),
            P(("dp", "seq"), None),
            P(("dp", "seq"), None, None),
            P(("dp", "seq"), None),
        ),
        check_vma=False,
    )
```

```python
import math

import jax
import jax.numpy as jnp
from jax import lax
from jax.experimental import pallas as pl
from jax.experimental.pallas import tpu as pltpu
from jax.sharding import PartitionSpec as P

HEADS = 12
HEAD_DIM = 64
EPS = 1e-06
NEG = -1000000000.0
BF16 = jnp.bfloat16
F32 = jnp.float32
ALL_VMEM = 62.6
FOLD = 112
ROWS = 208
NT = (((1,), (1,)), ((), ()))
TN = (((0,), (0,)), ((), ()))


def mm(a, b):
    return jnp.dot(a, b, preferred_element_type=F32)


def mm_nt(a, b):
    return lax.dot_general(a, b, NT, preferred_element_type=F32)


def mm_tn(a, b):
    return lax.dot_general(a, b, TN, preferred_element_type=F32)


def unit(values):
    center = values - jnp.mean(values, axis=-1, keepdims=True)
    spread = jnp.mean(center * center, axis=-1, keepdims=True)
    root = lax.rsqrt(spread + EPS)
    return center * root, root


def unit_back(scaled, rows, root):
    inner = jnp.mean(scaled * rows, axis=-1, keepdims=True)
    return root * (scaled - jnp.mean(scaled, axis=-1, keepdims=True) - rows * inner)


def lane_mask(index, width):
    lane = lax.broadcasted_iota(jnp.int32, (1, width), 1)
    return (lane >= index * HEAD_DIM) & (lane < (index + 1) * HEAD_DIM)


def image_length(mask_ref, counts_ref, image):
    which = lax.broadcasted_iota(jnp.int32, mask_ref.shape, 0)
    real = jnp.where(which == image, mask_ref[...], 0)
    total = jnp.sum(jnp.sum(real, axis=1, keepdims=True), axis=0, keepdims=True)
    return jnp.where(image < counts_ref[0], total, 0)


def kernel_call(
    kernel, ins, outs, scratch=(), limit=48, smem=(), hbm_in=(), hbm_out=(), flops=1
):
    kw = {
        "cost_estimate": pl.CostEstimate(flops=int(flops), bytes_accessed=0, transcendentals=0),
    }
    n_in, n_out, n_own = len(ins), len(outs), len(scratch)
    n_staged = len(hbm_in) + len(hbm_out)

    def wrapped(*refs):
        in_refs = list(refs[:n_in])
        out_refs = list(refs[n_in : n_in + n_out])
        own = refs[n_in + n_out : n_in + n_out + n_own]
        stages = refs[n_in + n_out + n_own :]
        reads, writes = [], {}
        for j, i in enumerate(hbm_in):
            reads.append(pltpu.make_async_copy(in_refs[i], stages[j], stages[-1].at[j]))
            in_refs[i] = stages[j]
        for j, i in enumerate(hbm_out, len(hbm_in)):
            writes[i] = pltpu.make_async_copy(stages[j], out_refs[i], stages[-1].at[j])
            out_refs[i] = stages[j]
        for copy in reads:
            copy.start()
        for copy in reads:
            copy.wait()
        kernel(*in_refs, *out_refs, *own)
        for copy in writes.values():
            copy.start()
        for copy in writes.values():
            copy.wait()

    def spec(i, staged):
        if i in staged:
            return pl.BlockSpec(memory_space=pltpu.HBM)
        return pl.BlockSpec(memory_space=pltpu.VMEM)

    in_specs = [
        pl.BlockSpec(memory_space=pltpu.SMEM) if i in smem else spec(i, hbm_in)
        for i in range(n_in)
    ]
    scratch = list(scratch)
    scratch += [pltpu.VMEM(ins[i].shape, ins[i].dtype) for i in hbm_in]
    scratch += [pltpu.VMEM(*outs[i]) for i in hbm_out]
    if n_staged:
        scratch.append(pltpu.SemaphoreType.DMA((n_staged,)))
    call = pl.pallas_call(
        wrapped,
        in_specs=in_specs,
        out_specs=[spec(i, hbm_out) for i in range(n_out)],
        out_shape=[jax.ShapeDtypeStruct(shape, kind) for shape, kind in outs],
        scratch_shapes=scratch,
        compiler_params=pltpu.CompilerParams(vmem_limit_bytes=int(limit * 2**20)),
        **kw,
    )
    return list(call(*ins))


def place(full, refs, dp):
    if len(refs) == 1:
        full[...] = refs[0][...]
        return
    part = refs[0].shape[0]
    half = part // 2

    def put(ref, rows, step, lo):
        at = pl.multiple_of((dp ^ step) * part + lo, half)
        full[pl.ds(at, rows.stop - rows.start), :] = ref[rows, :]

    whole, rest = slice(0, part), slice(part, part + half)
    for ref, step in zip(refs, (0, 1, 2, 4, 5, 6)):
        put(ref, whole, step, 0)
    put(refs[4], rest, 3, 0)
    put(refs[5], rest, 3, half)
    put(refs[6], slice(0, half), 7, 0)
    put(refs[7], slice(0, half), 7, half)


def forward_blocks(beside, across, far, y_ref, z_ref):
    part = far.shape[0]
    half = part // 2
    y_ref[:part, :] = far[...]
    y_ref[part:, :] = across[:half, :]
    z_ref[:part, :] = far[...]
    z_ref[part:, :] = beside[half:, :]


def forward_last(y_ref, z_ref, first_ref, second_ref):
    half = first_ref.shape[0]
    first_ref[...] = z_ref[:half, :]
    second_ref[...] = y_ref[half : 2 * half, :]


def head_masks(width, heads_here):
    return [lane_mask(h, width) for h in range(heads_here)]


def pack_inputs(groups, here, half, misc_w, experts):
    def kernel(*refs):
        qkv_ref, router_ref = refs[:2]
        vectors = refs[2:7]
        mix_ref, piece_ref, turn = refs[7:]
        seq = lax.axis_index("seq")
        features = qkv_ref.shape[1] // 3
        part = qkv_ref.shape[0]
        for g in range(groups):

            @pl.when(seq == g)
            def _():
                for j in range(3):
                    lo = j * features + g * here
                    piece_ref[:, j * here : (j + 1) * here] = qkv_ref[:, lo : lo + here]

        turn[...] = jnp.zeros_like(turn)
        turn[:experts, :part] = router_ref[...].astype(F32)
        for j in range(5):
            turn[experts + j : experts + j + 1, :part] = vectors[j][...].astype(F32)
        lo = 3 * here + misc_w
        piece_ref[:, 3 * here : lo] = turn[...].T[:part].astype(BF16)
        piece_ref[:, lo:] = mix_ref[:, pl.ds(pl.multiple_of((seq & 1) * half, 128), half)]

    return kernel


def by_image_owner(cot_ref, *cot_refs):
    seq = lax.axis_index("seq")
    for r in range(len(cot_refs)):
        cot_refs[r][...] = cot_ref[pl.ds(seq ^ r, 1)][0]


def normalize_tokens(groups):
    def kernel(*refs):
        tok_refs = refs[:groups]
        normed_ref, unit_ref, mine_ref, tok = refs[groups:]
        seq = lax.axis_index("seq")
        images, shard, _ = tok_refs[0].shape
        for r in range(groups):
            rows = pl.ds(pl.multiple_of((seq ^ r) * shard, shard), shard)
            tok[:, rows, :] = tok_refs[r][...]
        mine_ref[...] = tok[pl.ds(seq, 1), :ROWS, :][0]
        for i in range(images):
            normed, _ = unit(tok[i, :ROWS, :].astype(F32))
            normed_ref[i] = normed
            unit_ref[i] = normed.astype(BF16)

    return kernel


def attend_forward(groups, pieces, here, wide, misc_w, experts):
    heads_here = HEADS // groups

    def kernel(*refs):
        normed_ref, mask_ref, counts_ref = refs[:3]
        w_refs = refs[3 : 3 + pieces]
        sent_refs = refs[3 + pieces : 3 + pieces + groups]
        rest = refs[3 + pieces + groups :]
        (half_ref, probs_ref, xa_ref, qkv_ref, wpad_ref, rows_ref, router_ref, dense, heads) = rest
        seq = lax.axis_index("seq")
        images, _, features = normed_ref.shape
        place(dense, w_refs, lax.axis_index("dp"))
        wpad_ref[...] = jnp.zeros_like(wpad_ref)
        for j in range(3):
            wpad_ref[:, j * wide : j * wide + here] = dense[:, j * here : (j + 1) * here]
        half_ref[...] = dense[:, 3 * here + misc_w :]
        misc = dense[:, 3 * here : 3 * here + misc_w]
        router_ref[...] = misc[:, :experts]
        rows_ref[...] = misc.astype(F32).T[experts : experts + 8]
        xa_ref[...] = (normed_ref[...] * rows_ref[0:1][None] + rows_ref[1:2][None]).astype(BF16)
        flat = xa_ref[...].reshape(images * ROWS, features)
        qkv_ref[:, :ROWS, :] = (
            mm(flat, wpad_ref[...]).astype(BF16).reshape(images, ROWS, 3 * wide)
        )
        keys = qkv_ref.shape[1]
        qkv_ref[:, ROWS:, :] = jnp.zeros((images, keys - ROWS, 3 * wide), BF16)
        place_of_key = lax.broadcasted_iota(jnp.int32, (1, keys), 1)
        for i in range(images):
            valid = place_of_key < image_length(mask_ref, counts_ref, i)
            q, k, v = head_stacks(qkv_ref, i, wide, heads_here)
            scores = mm_nt(q, k) * HEAD_DIM ** (-0.5)
            for h in range(heads_here):
                lanes = slice(h * keys, (h + 1) * keys)
                masked = jnp.where(valid, scores[:, lanes], NEG)
                top = jnp.exp(masked - jnp.max(masked, axis=-1, keepdims=True))
                total = jnp.sum(top, axis=-1, keepdims=True)
                probs_ref[i, :, lanes] = (top / total).astype(BF16)
            heads[i] = mm(probs_ref[i], v)[:, :here].astype(BF16)
        for r in range(groups):
            fold(sent_refs[r], heads[pl.ds(seq ^ r, 1)][0])

    return kernel


def head_stacks(qkv_ref, image, wide, heads_here):
    masks = head_masks(wide, heads_here)
    stacks = []
    for j in (1, 2):
        rows = qkv_ref[image, :, j * wide : (j + 1) * wide]
        stacks.append(jnp.concatenate([jnp.where(m, rows, jnp.zeros_like(rows)) for m in masks]))
    return qkv_ref[image, :ROWS, :wide], stacks[0], stacks[1]


def fold(ref, rows):
    top, width = ref.shape[0], rows.shape[1]
    ref[:, :width] = rows[:top]
    ref[: rows.shape[0] - top, width:] = rows[top:]


def unfold(ref, part, count):
    width = ref.shape[1] // 2
    if part == 0:
        return ref[:, :width]
    return ref[: count - ref.shape[0], width:]


def head_rows(seq, r, here):
    return pl.ds(pl.multiple_of((seq ^ r) * here, here), here)


def route_forward(groups, here, half):
    def kernel(*refs):
        sent_refs = refs[:groups]
        cot_refs = refs[groups : 2 * groups]
        mine_ref, rows_ref, router_ref, mask_ref, counts_ref = refs[2 * groups : 2 * groups + 5]
        half_refs = refs[2 * groups + 5 : -8]
        slots_ref, resid_ref, mixed_ref, logits_ref, mix_ref, grad_ref, heads_ref, cot = refs[-8:]
        seq = lax.axis_index("seq")
        for j in range(2):
            lanes = pl.ds(pl.multiple_of(((seq & 1) ^ j) * half, 128), half)
            mix_ref[:, lanes] = half_refs[j][...]
        for r in range(groups):
            heads_ref[r, :FOLD] = unfold(sent_refs[r], 0, ROWS)
            heads_ref[r, FOLD:] = unfold(sent_refs[r], 1, ROWS)
            shard = cot_refs[r].shape[0]
            cot[pl.ds(pl.multiple_of((seq ^ r) * shard, shard), shard), :] = cot_refs[r][...]
        resid = mine_ref[...].astype(F32) + rows_ref[2:3]
        for r in range(groups):
            resid = resid + mm(heads_ref[r], mix_ref[head_rows(seq, r, here), :])
        resid_ref[...] = resid
        normed, _ = unit(resid)
        mixed = (normed * rows_ref[3:4] + rows_ref[4:5]).astype(BF16)
        mixed_ref[...] = mixed
        logits = mm(mixed, router_ref[...])
        logits_ref[...] = logits
        length = image_length(mask_ref, counts_ref, seq)
        valid = lax.broadcasted_iota(jnp.int32, (ROWS, 1), 0) < length
        dispatch = token_softmax(logits, valid)
        combine = slot_softmax(logits)
        grad = cot[:ROWS, :]
        grad = jnp.where(valid, grad, jnp.zeros_like(grad))
        grad_ref[...] = grad
        slots_ref[:, 0, :] = mm_tn(dispatch.astype(BF16), mixed).astype(BF16)
        slots_ref[:, 1, :] = mm_tn(combine.astype(BF16), grad).astype(BF16)

    return kernel


def token_softmax(logits, valid):
    masked = jnp.where(valid, logits, NEG)
    top = jnp.exp(masked - jnp.max(masked, axis=0, keepdims=True))
    return top / jnp.sum(top, axis=0, keepdims=True)


def slot_softmax(logits):
    top = jnp.exp(logits - jnp.max(logits, axis=-1, keepdims=True))
    return top / jnp.sum(top, axis=-1, keepdims=True)


def expert_values(
    x_ref, win_ref, bias_ref, wout_ref, obias_ref, back_ref, hid_ref, pre_ref, hb_ref, ob_ref
):
    x = x_ref[:, 0, :]
    g = x_ref[:, 1, :]
    ob_ref[...] = jnp.sum(g.astype(F32), axis=0, keepdims=True)
    pre = mm(x, win_ref[0]) + bias_ref[...].astype(F32)
    phi = 0.5 * (1.0 + lax.erf(pre * 2.0 ** (-0.5)))
    hidden = (pre * phi).astype(BF16)
    hid_ref[...] = hidden
    back_ref[:, 0, :] = (mm(hidden, wout_ref[0]) + obias_ref[...].astype(F32)).astype(BF16)
    slope = phi + pre * jnp.exp(-0.5 * pre * pre) * (2.0 * math.pi) ** (-0.5)
    grad_pre = (mm_nt(g, wout_ref[0]) * slope).astype(BF16)
    pre_ref[...] = grad_pre
    hb_ref[...] = jnp.sum(grad_pre.astype(F32), axis=0, keepdims=True)
    back_ref[:, 1, :] = mm_nt(grad_pre, win_ref[0]).astype(BF16)


def expert_weights(x_ref, hid_ref, pre_ref, *refs):
    gin_ref, gout_ref = refs[-2:]
    gin_ref[0] = mm_tn(x_ref[:, 0, :], pre_ref[...])
    gout_ref[0] = mm_tn(hid_ref[...], x_ref[:, 1, :])


def route_backward(groups, here, misc_w, experts):
    def kernel(*refs):
        (back_ref, resid_ref, mixed_ref, logits_ref, grad_ref, mix_ref, router_ref, rows_ref) = (
            refs[:8]
        )
        mask_ref, counts_ref = refs[8:10]
        heads_ref = refs[10]
        rest = refs[11:]
        gheads_refs = rest[:groups]
        tok, keep_ref, send_ref, misc_ref, full, turn = rest[groups:]
        seq = lax.axis_index("seq")
        length = image_length(mask_ref, counts_ref, seq)
        valid = lax.broadcasted_iota(jnp.int32, (ROWS, 1), 0) < length
        logits = logits_ref[...]
        dispatch = token_softmax(logits, valid)
        combine = slot_softmax(logits)
        resid = resid_ref[...]
        mixed = mixed_ref[...]
        slot_out = back_ref[:, 0, :]
        grad_slot = back_ref[:, 1, :]
        grad = grad_ref[...]
        out = jnp.where(valid, resid + mm(combine.astype(BF16), slot_out), 0.0).astype(BF16)
        grad_combine = mm_nt(grad, slot_out)
        grad_dispatch = mm_nt(mixed, grad_slot)
        grad_logits = combine * (
            grad_combine - jnp.sum(combine * grad_combine, axis=-1, keepdims=True)
        ) + dispatch * (grad_dispatch - jnp.sum(dispatch * grad_dispatch, axis=0, keepdims=True))
        low = grad_logits.astype(BF16)
        grad_mixed = mm(dispatch.astype(BF16), grad_slot) + mm_nt(low, router_ref[...])
        normed, root = unit(resid)
        turn[...] = jnp.zeros_like(turn)
        turn[experts + 3 : experts + 4, :] = jnp.sum(grad_mixed * normed, axis=0, keepdims=True)
        turn[experts + 4 : experts + 5, :] = jnp.sum(grad_mixed, axis=0, keepdims=True)
        grad_resid = grad.astype(F32) + unit_back(grad_mixed * rows_ref[3:4], normed, root)
        turn[experts + 2 : experts + 3, :] = jnp.sum(grad_resid, axis=0, keepdims=True)
        turn[:experts, :] = mm_tn(low, mixed)
        misc_ref[...] = turn[...]
        gr = grad_resid.astype(BF16)
        tok[...] = jnp.zeros_like(tok)
        tok[0, :ROWS, :] = out
        tok[1, :ROWS, :] = gr
        for r in range(groups):
            fold(gheads_refs[r], mm_nt(gr, mix_ref[head_rows(seq, r, here), :]).astype(BF16))
            full[head_rows(seq, r, here), :] = mm_tn(heads_ref[r], gr).astype(BF16)
        for core in range(2):

            @pl.when((seq & 1) == core)
            def _():
                for j in range(groups // 2):
                    lanes = slice(j * here, (j + 1) * here)
                    lo = (2 * j + core) * here
                    keep_ref[:, lanes] = full[:, lo : lo + here]
                    lo = (2 * j + 1 - core) * here
                    send_ref[:, lanes] = full[:, lo : lo + here]

    return kernel


def add_shares(parts, size):
    def kernel(keep_ref, got_ref, *refs):
        mine_refs, send_refs = refs[: len(parts)], refs[len(parts) : -1]
        total = refs[-1]
        total[...] = (keep_ref[...].astype(F32) + got_ref[...].astype(F32)).astype(BF16)
        chip = lax.axis_index("seq") // 2
        dp = lax.axis_index("dp")
        width = mine_refs[0].shape[1]

        def block(step, lanes):
            if size == total.shape[0]:
                return total[:, lanes]
            return total[pl.ds(pl.multiple_of((dp ^ step) * size, size), size), lanes]

        for j in range(2):

            @pl.when(chip == j)
            def _():
                own, other = (slice(to * width, (to + 1) * width) for to in (j, 1 - j))
                for steps, mine, send in zip(parts, mine_refs, send_refs):
                    for k, step in enumerate(steps):
                        mine[k * size : (k + 1) * size, :] = block(step, own)
                    fold(send, jnp.concatenate([block(step, other) for step in steps]))

    return kernel


def both_chips(mine_ref, other_ref):
    count, half = mine_ref.shape[0], other_ref.shape[0]
    return jnp.concatenate(
        [
            mine_ref[:half, :].astype(F32) + unfold(other_ref, 0, count).astype(F32),
            mine_ref[half:, :].astype(F32) + unfold(other_ref, 1, count).astype(F32),
        ]
    )


def image_backward(gheads_ref, image, qkv_ref, probs_ref, gqkv, gh, gs, heads_here):
    keys = qkv_ref.shape[1]
    wide = gh.shape[1]
    here = gheads_ref.shape[1] // 2
    masks = head_masks(wide, heads_here)
    scaling = HEAD_DIM ** (-0.5)
    gh[:FOLD, :here] = unfold(gheads_ref, 0, ROWS)
    gh[FOLD:, :here] = unfold(gheads_ref, 1, ROWS)

    def by_head(stacked):
        picked = stacked[(heads_here - 1) * keys : (heads_here - 1) * keys + ROWS]
        for h in range(heads_here - 1):
            picked = jnp.where(masks[h], stacked[h * keys : h * keys + ROWS], picked)
        return picked

    q, k, v = head_stacks(qkv_ref, image, wide, heads_here)
    go = gh[...]
    gp = mm_nt(go, v)
    for h in range(heads_here):
        lanes = slice(h * keys, (h + 1) * keys)
        probs = probs_ref[image, :, lanes].astype(F32)
        inner = jnp.sum(probs * gp[:, lanes], axis=-1, keepdims=True)
        gs[:, lanes] = (probs * (gp[:, lanes] - inner)).astype(BF16)
    rows = pl.ds(pl.multiple_of(image * ROWS, ROWS), ROWS)
    gqkv[rows, :wide] = (mm(gs[...], k) * scaling).astype(BF16)
    gqkv[rows, wide : 2 * wide] = (by_head(mm_tn(gs[...], q)) * scaling).astype(BF16)
    gqkv[rows, 2 * wide :] = by_head(mm_tn(probs_ref[image], go)).astype(BF16)


def attend_backward_near(heads_here):
    def kernel(own_ref, near_ref, qkv_ref, probs_ref, gqkv, gh, gs):
        seq = lax.axis_index("seq")
        gh[...] = jnp.zeros_like(gh)
        for r, ref in enumerate((own_ref, near_ref)):
            image_backward(ref, seq ^ r, qkv_ref, probs_ref, gqkv, gh, gs, heads_here)

    return kernel


def attend_backward_far(groups, here, wide, misc_w, experts):
    heads_here = HEADS // groups

    def kernel(*refs):
        gheads_refs = refs[: groups - 2]
        qkv_ref, probs_ref, xa_ref, unit_ref, wpad_ref, misc_ref, token_ref = refs[
            groups - 2 : groups + 5
        ]
        done_ref, gqkv, keep_ref, send_ref, gw_ref, gh, gs, gxs, turn = refs[groups + 5 :]
        images, _, features = unit_ref.shape
        seq = lax.axis_index("seq")
        gh[...] = jnp.zeros_like(gh)
        for r in range(2):
            rows = pl.ds(pl.multiple_of((seq ^ r) * ROWS, ROWS), ROWS)
            gqkv[rows, :] = done_ref[rows, :]
        for j, ref in enumerate(gheads_refs):
            image_backward(ref, seq ^ (j + 2), qkv_ref, probs_ref, gqkv, gh, gs, heads_here)
        gx = mm_nt(gqkv[...], wpad_ref[...])
        shard = keep_ref.shape[2]
        gxs[:, :ROWS, :] = gx.astype(BF16).reshape(images, ROWS, features)
        gxs[:, ROWS:, :] = jnp.zeros((images, gxs.shape[1] - ROWS, features), BF16)
        for j in range(2):
            for to, ref in ((seq ^ (2 * j), keep_ref), (seq ^ (2 * j + 1), send_ref)):
                rows = pl.ds(pl.multiple_of(to * shard, shard), shard)
                ref[j, :images] = gxs[:, rows, :]
                ref[j, images:] = token_ref[:, rows, :]
        normed = unit_ref[...].reshape(images * ROWS, features).astype(F32)
        turn[...] = misc_ref[...]
        turn[experts : experts + 1, :] = jnp.sum(gx * normed, axis=0, keepdims=True)
        turn[experts + 1 : experts + 2, :] = jnp.sum(gx, axis=0, keepdims=True)
        gw_ref[:, 3 * here :] = turn[...].T.astype(BF16)
        gw = mm_tn(xa_ref[...].reshape(images * ROWS, features), gqkv[...]).astype(BF16)
        for j in range(3):
            gw_ref[:, j * here : (j + 1) * here] = gw[:, j * wide : j * wide + here]

    return kernel


def cut_gradients(gw_ref, mine_ref, other_ref, *out_refs):
    width = gw_ref.shape[1]
    gmix = both_chips(mine_ref, other_ref).astype(BF16)
    if len(out_refs) == 1:
        out_refs[0][:, :width] = gw_ref[...]
        out_refs[0][:, width:] = gmix
        return
    dp = lax.axis_index("dp")
    part = out_refs[0].shape[0]
    half = part // 2

    def put(ref, at, step, k, lo, rows):
        source = pl.multiple_of((dp ^ step) * part + lo, half)
        ref[at : at + rows, :width] = gw_ref[pl.ds(source, rows), :]
        if k is not None:
            ref[at : at + rows, width:] = gmix[k * part + lo : k * part + lo + rows]

    for ref, step in zip(out_refs, (0, 1, 2, 4)):
        put(ref, 0, step, None, 0, part)
    put(out_refs[4], 0, 5, 1, 0, part)
    put(out_refs[4], part, 3, 3, 0, half)
    put(out_refs[5], 0, 6, 2, 0, part)
    put(out_refs[5], part, 3, 3, half, half)
    put(out_refs[6], 0, 7, 0, 0, half)
    put(out_refs[7], 0, 7, 0, half, half)


def token_backward(keep_ref, core_ref, chip_ref, tok_ref, rows_ref, out_ref, grad_ref, resid):
    seq = lax.axis_index("seq")
    images, shard, features = tok_ref.shape
    total = keep_ref[0, :images].astype(F32) + core_ref[0, :images].astype(F32)
    total = (total + chip_ref[:images].astype(F32)).reshape(images * shard, features)
    for r, got in enumerate(
        (keep_ref.at[0, images:], core_ref.at[0, images:], chip_ref.at[images : images + 2],
         chip_ref.at[images + 2 :])
    ):
        out_ref[pl.ds(seq ^ r, 1)] = got[0:1]
        resid[pl.ds(seq ^ r, 1)] = got[1:2]
    normed, root = unit(tok_ref[...].astype(F32).reshape(images * shard, features))
    back = unit_back(total * rows_ref[0:1], normed, root).reshape(images, shard, features)
    grad_ref[...] = (resid[...].astype(F32) + back).astype(BF16)


def plus(a, b):
    return (a.astype(F32) + b.astype(F32)).astype(BF16)


def reduce_last(y_ref, z_ref, first_ref, second_ref, to_y, to_z):
    half = first_ref.shape[0]
    to_y[...] = y_ref[...]
    to_z[...] = z_ref[...]
    to_y[half : 2 * half, :] = plus(y_ref[half : 2 * half, :], second_ref[...])
    to_z[:half, :] = plus(z_ref[:half, :], first_ref[...])


def reduce_blocks(
    own_ref, beside_ref, across_ref, far_ref, y_ref, z_ref, mine_ref, other_ref,
    own, beside, across, far,
):
    part = far_ref.shape[0]
    half = part // 2
    gmix = both_chips(mine_ref, other_ref)
    width = far_ref.shape[1] - gmix.shape[1]

    def block(ref, k):
        return jnp.concatenate(
            [ref[:, :width].astype(F32), gmix[k * part : (k + 1) * part]], axis=1
        )

    beside_sum, across_sum, far_sum, own_sum = (
        block(ref, k) for k, ref in enumerate((beside_ref, across_ref, far_ref, own_ref))
    )
    own[...] = own_sum.astype(BF16)
    far_sum = far_sum + y_ref[:part, :].astype(F32) + z_ref[:part, :].astype(F32)
    far[...] = far_sum.astype(BF16)
    across[:half, :] = (across_sum[:half] + y_ref[part:, :].astype(F32)).astype(BF16)
    across[half:, :] = across_sum[half:].astype(BF16)
    beside[:half, :] = beside_sum[:half].astype(BF16)
    beside[half:, :] = (beside_sum[half:] + z_ref[part:, :].astype(F32)).astype(BF16)


def add_second(keep_ref, got_ref, out_ref):
    images = keep_ref.shape[1] - 2
    out_ref[:images] = (
        keep_ref[1, :images].astype(F32) + got_ref[1, :images].astype(F32)
    ).astype(BF16)
    out_ref[images : images + 2] = keep_ref[1, images:]
    out_ref[images + 2 :] = got_ref[1, images:]


def sum_parts(*refs):
    total = refs[0][...].astype(F32)
    for ref in refs[1:-1]:
        total = total + ref[...].astype(F32)
    refs[-1][...] = total.astype(BF16)


def spread_parts(groups, here, misc_w, experts):
    def kernel(*refs):
        in_refs = refs[:groups]
        qkv_ref, mix_ref, router_ref = refs[groups : groups + 3]
        row_refs = refs[groups + 3 :]
        features = mix_ref.shape[1]
        seq = lax.axis_index("seq")
        for s in range(groups):

            @pl.when(seq == s)
            def _():
                for r in range(groups):
                    g = s ^ r
                    for j in range(3):
                        lo = j * features + g * here
                        part = in_refs[r][:, j * here : (j + 1) * here]
                        qkv_ref[:, lo : lo + here] = part.astype(F32)
                    part = in_refs[r][:, 3 * here + misc_w :]
                    mix_ref[:, g * here : (g + 1) * here] = part.astype(F32)

        misc = in_refs[0][:, 3 * here : 3 * here + misc_w].astype(F32)
        for r in range(1, groups):
            misc = misc + in_refs[r][:, 3 * here : 3 * here + misc_w].astype(F32)
        misc = misc.T
        router_ref[...] = misc[:experts]
        for j in range(5):
            row_refs[j][...] = misc[experts + j : experts + j + 1]

    return kernel


def body(
    tokens,
    pad_mask,
    counts,
    attn_gain,
    attn_shift,
    qkv_weight,
    mix_weight,
    mix_bias,
    moe_gain,
    moe_shift,
    router,
    expert_in,
    hidden_bias,
    expert_out,
    output_bias,
    cotangent,
):
    images, shard, features = tokens.shape
    groups = lax.axis_size("seq")
    lanes = lax.axis_size("dp")
    devices = groups * lanes
    part = mix_weight.shape[0]
    experts = router.shape[1]
    hidden = expert_in.shape[2]
    misc_w = -(-(experts + 8) // 64) * 64
    here = HEADS // groups * HEAD_DIM
    wide = -(-here // 128) * 128
    half = features // 2
    full = groups * shard
    direct = lanes == 8 and part % 32 == 0
    piece_w = 3 * here + misc_w + here

    def swap(a, axis, step):
        return lax.ppermute(a, axis, [(i, i ^ step) for i in range(lax.axis_size(axis))])

    def exchange(parts):
        moved = {r: swap(parts[r], "seq", r) for r in range(groups - 1, 0, -1)}
        return [parts[0]] + [moved[r] for r in range(1, groups)]

    packed_w = 3 * here + misc_w + half
    (piece,) = kernel_call(
        pack_inputs(groups, here, half, misc_w, experts),
        [qkv_weight, router.T]
        + [v.reshape(1, part) for v in (attn_gain, attn_shift, mix_bias, moe_gain, moe_shift)]
        + [mix_weight],
        [((part, packed_w), BF16)],
        [pltpu.VMEM((misc_w, -(-part // 128) * 128), F32)],
        limit=ALL_VMEM,
        hbm_in=tuple(range(8)),
    )
    cots = exchange(
        kernel_call(by_image_owner, [cotangent], [((shard, features), BF16)] * groups, limit=4)
    )
    over = swap(tokens, "seq", 2)
    near = swap(tokens, "seq", 1)
    if direct:
        far, across, beside = (swap(piece, "dp", step) for step in (4, 2, 1))
        far, across, beside, over, cots[2] = lax.optimization_barrier(
            (far, across, beside, over, cots[2])
        )
        longer = ((part + part // 2, packed_w), BF16)
        to_y, to_z = kernel_call(forward_blocks, [beside, across, far], [longer] * 2, limit=4)
        by_y, by_z = swap(to_y, "dp", 1), swap(to_z, "dp", 2)
        by_y, by_z, near, cots[1], cots[3] = lax.optimization_barrier(
            (by_y, by_z, near, cots[1], cots[3])
        )
        a, b = kernel_call(forward_last, [by_y, by_z], [((part // 2, packed_w), BF16)] * 2, limit=4)
        piece_parts = [piece, beside, across, far, by_y, by_z, swap(a, "dp", 1), swap(b, "dp", 2)]
    else:
        piece_parts = [lax.all_gather(piece, "dp", axis=0, tiled=True)]
    normed, units, mine = kernel_call(
        normalize_tokens(groups),
        [tokens, near, over, swap(over, "seq", 1)],
        [
            ((images, ROWS, features), F32),
            ((images, ROWS, features), BF16),
            ((ROWS, features), BF16),
        ],
        [pltpu.VMEM((images, full, features), BF16)],
        limit=8,
        flops=1e8,
    )
    outs = kernel_call(
        attend_forward(groups, len(piece_parts), here, wide, misc_w, experts),
        [normed, pad_mask, counts] + piece_parts,
        [((FOLD, 2 * here), BF16)] * groups
        + [
            ((features, half), BF16),
            ((images, ROWS, HEADS // groups * full), BF16),
            ((images, ROWS, features), BF16),
            ((images, full, 3 * wide), BF16),
            ((features, 3 * wide), BF16),
            ((8, features), F32),
            ((features, experts), BF16),
        ],
        [
            pltpu.VMEM((features, packed_w), BF16),
            pltpu.VMEM((images, ROWS, here), BF16),
        ],
        smem=(2,),
        limit=16,
        flops=1e8,
    )
    sent = exchange(outs[:groups])
    mix_half, probs, xa, qkv, wpad, rows, router_full = outs[groups:]
    slots, resid, mixed, logits, mix_full, grad, heads = kernel_call(
        route_forward(groups, here, half),
        sent
        + cots
        + [mine, rows, router_full, pad_mask, counts, mix_half, swap(mix_half, "seq", 1)],
        [
            ((experts, 2, features), BF16),
            ((ROWS, features), F32),
            ((ROWS, features), BF16),
            ((ROWS, experts), F32),
            ((features, features), BF16),
            ((ROWS, features), BF16),
            ((groups, ROWS, here), BF16),
        ],
        [pltpu.VMEM((full, features), BF16)],
        smem=(2 * groups + 4,),
        limit=10,
        flops=5e9,
    )
    slots = lax.all_to_all(slots, ("dp", "seq"), split_axis=0, concat_axis=0, tiled=True)
    block = min(512, hidden)
    back, hid, grad_pre, grad_hidden_bias, grad_output_bias = kernel_call(
        expert_values,
        [slots, expert_in, hidden_bias, expert_out, output_bias],
        [
            ((devices, 2, features), BF16),
            ((devices, hidden), BF16),
            ((devices, hidden), BF16),
            ((1, hidden), F32),
            ((1, features), F32),
        ],
        limit=8,
        flops=5e9,
    )
    back = lax.all_to_all(back, ("dp", "seq"), split_axis=0, concat_axis=0, tiled=True)

    def expert_gradients(first, count, ins):
        lane_spec = pl.BlockSpec((devices, block), lambda i: (0, i + first))
        return pl.pallas_call(
            expert_weights,
            grid=(count,),
            in_specs=[pl.BlockSpec((devices, 2, features), lambda i: (0, 0, 0))]
            + [lane_spec] * 2
            + [pl.BlockSpec(memory_space=pl.ANY)] * (len(ins) - 3),
            out_specs=[
                pl.BlockSpec((1, features, block), lambda i: (0, 0, i + first)),
                pl.BlockSpec((1, block, features), lambda i: (0, i + first, 0)),
            ],
            out_shape=[
                jax.ShapeDtypeStruct((1, features, hidden), F32),
                jax.ShapeDtypeStruct((1, hidden, features), F32),
            ],
            input_output_aliases={i: i - 3 for i in range(3, len(ins))},
            compiler_params=pltpu.CompilerParams(vmem_limit_bytes=12 * 2**20),
            cost_estimate=pl.CostEstimate(
                flops=1 if first else 10**11, bytes_accessed=0, transcendentals=0
            ),
        )(*ins)

    steps = hidden // block
    early = steps // 3
    expert_grads = expert_gradients(0, early, [slots, hid, grad_pre])
    outs = kernel_call(
        route_backward(groups, here, misc_w, experts),
        [back, resid, mixed, logits, grad, mix_full, router_full, rows, pad_mask, counts, heads],
        [((FOLD, 2 * here), BF16)] * groups
        + [((2, full, features), BF16)]
        + [((features, groups // 2 * here), BF16)] * 2
        + [((misc_w, features), F32)],
        [pltpu.VMEM((features, features), BF16), pltpu.VMEM((misc_w, features), F32)],
        smem=(9,),
        limit=16,
        flops=5e9,
    )
    gheads = exchange(outs[:groups])
    token_rows, keep, send, misc = outs[groups:]
    mix_parts = ((7, 5, 6, 3), (1, 2, 4, 0)) if direct else ((0,),)
    size = part if direct else features
    count = size * len(mix_parts[0])
    outs_mix = kernel_call(
        add_shares(mix_parts, size),
        [keep, swap(send, "seq", 1)],
        [((count, here), BF16)] * len(mix_parts)
        + [((count // 2, 2 * here), BF16)] * len(mix_parts),
        [pltpu.VMEM((features, groups // 2 * here), BF16)],
        limit=8,
    )
    *outs_mix, own = lax.optimization_barrier(outs_mix + [gheads[0]])
    gmix, gmix_send = outs_mix[: len(mix_parts)], outs_mix[len(mix_parts) :]
    gmix_other = [swap(gmix_send[0], "seq", 2)]
    gqkv_spec = ((images * ROWS, 3 * wide), BF16)
    image_scratch = [
        pltpu.VMEM((ROWS, wide), BF16),
        pltpu.VMEM((ROWS, HEADS // groups * full), BF16),
    ]
    (gqkv,) = kernel_call(
        attend_backward_near(HEADS // groups),
        [own, gheads[1], qkv, probs],
        [gqkv_spec],
        image_scratch,
        limit=8,
        flops=1e10,
    )
    gqkv, gx, gx_send, gw = kernel_call(
        attend_backward_far(groups, here, wide, misc_w, experts),
        gheads[2:] + [qkv, probs, xa, units, wpad, misc, token_rows, gqkv],
        [
            gqkv_spec,
            ((2, images + 2, shard, features), BF16),
            ((2, images + 2, shard, features), BF16),
            ((features, 3 * here + misc_w), BF16),
        ],
        image_scratch
        + [
            pltpu.VMEM((images, full, features), BF16),
            pltpu.VMEM((misc_w, features), F32),
        ],
        limit=20,
        flops=1e10,
    )
    gx_core = swap(gx_send, "seq", 1)
    whole = ((part, piece_w), BF16)
    longer = ((part + part // 2, piece_w), BF16)
    shorter = ((part // 2, piece_w), BF16)
    out_parts = [whole] * 4 + [longer] * 2 + [shorter] * 2
    if not direct:
        out_parts = [((features, piece_w), BF16)]
    outs = kernel_call(
        cut_gradients,
        [gw, gmix[0], gmix_other[0]],
        out_parts,
        limit=8,
        flops=2e10,
    )
    gx_core, _ = lax.optimization_barrier((gx_core, outs[0]))
    if direct:
        own, beside, across, far, to_y, to_z, first, second = outs
        first, second = swap(first, "dp", 1), swap(second, "dp", 2)
        late, _ = lax.optimization_barrier((gmix_send[1], gmix_other[0]))
        first, second, late, *expert_grads = lax.optimization_barrier(
            [first, second, swap(late, "seq", 2)] + list(expert_grads)
        )
        expert_grads = expert_gradients(early, steps - early, [slots, hid, grad_pre, *expert_grads])
        to_y, to_z = kernel_call(
            reduce_last, [to_y, to_z, first, second], [longer] * 2, limit=4
        )
        by_y, by_z = swap(to_y, "dp", 1), swap(to_z, "dp", 2)
        by_y, by_z, *expert_grads = lax.optimization_barrier([by_y, by_z] + list(expert_grads))
        own, beside, across, far = kernel_call(
            reduce_blocks,
            [own, beside, across, far, by_y, by_z, gmix[1], late],
            [whole] * 4,
            limit=8,
        )
        sums = [swap(far, "dp", 4), swap(across, "dp", 2), swap(beside, "dp", 1), own]
    else:
        expert_grads = expert_gradients(early, steps - early, [slots, hid, grad_pre, *expert_grads])
        arrived = lax.all_to_all(outs[0], "dp", split_axis=0, concat_axis=0, tiled=True)
        sums = [arrived[r * part : (r + 1) * part] for r in range(lanes)]
    (gx_sum,) = kernel_call(
        add_second, [gx, gx_core], [((images + 4, shard, features), BF16)], limit=4
    )
    gx_chip = swap(gx_sum, "seq", 2)
    (share,) = kernel_call(sum_parts, sums, [whole], limit=4)
    share, gx_chip = lax.optimization_barrier((share, gx_chip))
    block_out, input_grad = kernel_call(
        token_backward,
        [gx, gx_core, gx_chip, tokens, rows],
        [((images, shard, features), BF16), ((images, shard, features), BF16)],
        [pltpu.VMEM((images, shard, features), BF16)],
        limit=8,
        flops=2e9,
    )
    share_over = swap(share, "seq", 2)
    shares = [share, swap(share, "seq", 1), share_over, swap(share_over, "seq", 1)]
    grad_qkv, grad_mix, grad_router, *vector_rows = kernel_call(
        spread_parts(groups, here, misc_w, experts),
        shares,
        [((part, 3 * features), F32), ((part, features), F32), ((experts, part), F32)]
        + [((1, part), F32)] * 5,
        limit=8,
    )
    vector_rows = [v.reshape(part) for v in vector_rows]
    return (
        block_out,
        input_grad,
        vector_rows[0],
        vector_rows[1],
        grad_qkv,
        grad_mix,
        vector_rows[2],
        vector_rows[3],
        vector_rows[4],
        grad_router.T,
        expert_grads[0],
        grad_hidden_bias,
        expert_grads[1],
        grad_output_bias,
    )


def solution(mesh):
    return jax.shard_map(
        body,
        mesh=mesh,
        in_specs=(
            P("dp", "seq", None),
            P("dp", None),
            P("dp"),
            P("dp"),
            P("dp"),
            P("dp", None),
            P("dp", None),
            P("dp"),
            P("dp"),
            P("dp"),
            P("dp", None),
            P(("dp", "seq"), None, None),
            P(("dp", "seq"), None),
            P(("dp", "seq"), None, None),
            P(("dp", "seq"), None),
            P("dp", "seq", None),
        ),
        out_specs=(
            P("dp", "seq", None),
            P("dp", "seq", None),
            P("dp"),
            P("dp"),
            P("dp", None),
            P("dp", None),
            P("dp"),
            P("dp"),
            P("dp"),
            P("dp", None),
            P(("dp", "seq"), None, None),
            P(("dp", "seq"), None),
            P(("dp", "seq"), None, None),
            P(("dp", "seq"), None),
        ),
        check_vma=False,
    )
```
